32 devices in a mesh: dp: 32 (over z, y, x, core).
Axes of the slice: x: 2, y: 2, z: 4, core: 2. Of those that a mesh axis runs over, the one named last changes fastest.
Arguments:
- tokens: bfloat16 [32768, 1024], P('dp'), may hold values from -6 to 6
- cotangent: bfloat16 [32768, 1024], P('dp'), may hold values from -6 to 6
- w_qkv: bfloat16 [1024, 3072], P('dp'), may hold values from -0.1875 to 0.1875
- q_bias: bfloat16 [1024], P('dp'), may hold values from -2 to 2
- v_bias: bfloat16 [1024], P('dp'), may hold values from -2 to 2
- w_out: bfloat16 [1024, 1024], P('dp'), may hold values from -0.75 to 0.75
- out_bias: bfloat16 [1024], P('dp'), may hold values from -2 to 2
- attn_gain: bfloat16 [1024], P('dp'), may hold values from 0.5 to 1.5
- attn_shift: bfloat16 [1024], P('dp'), may hold values from -2 to 2
- w_up: bfloat16 [1024, 4096], P('dp'), may hold values from -0.1875 to 0.1875
- up_bias: bfloat16 [4096], P('dp'), may hold values from -2 to 2
- w_down: bfloat16 [4096, 1024], P('dp'), may hold values from -0.1875 to 0.1875
- down_bias: bfloat16 [1024], P('dp'), may hold values from -2 to 2
- mlp_gain: bfloat16 [1024], P('dp'), may hold values from 0.5 to 1.5
- mlp_shift: bfloat16 [1024], P('dp'), may hold values from -2 to 2
Outputs:
- layer_out: bfloat16 [32768, 1024], P('dp')
- input_grad: bfloat16 [32768, 1024], P('dp')
- w_qkv_grad: float32 [1024, 3072], P('dp')
- q_bias_grad: float32 [1024], P('dp')
- v_bias_grad: float32 [1024], P('dp')
- w_out_grad: float32 [1024, 1024], P('dp')
- out_bias_grad: float32 [1024], P('dp')
- attn_gain_grad: float32 [1024], P('dp')
- attn_shift_grad: float32 [1024], P('dp')
- w_up_grad: float32 [1024, 4096], P('dp')
- up_bias_grad: float32 [4096], P('dp')
- w_down_grad: float32 [4096, 1024], P('dp')
- down_bias_grad: float32 [1024], P('dp')
- mlp_gain_grad: float32 [1024], P('dp')
- mlp_shift_grad: float32 [1024], P('dp')
The draws below stay inside these ranges and needn't reach their ends.
All inputs are finite; a program needn't handle non-finite values.
Results may differ from the reference program's by a relative error of at most 0.015.
Values may be sent and summed in bfloat16 or wider, within the bound.
No kernel may reach another device: no remote copies, remote signals or barrier semaphores. Data moves between devices by JAX's collectives and lax.ppermute only.
A program may use at most 256 MiB of HBM per device.

```python
import math
import jax
import jax.numpy as jnp
from jax import lax

D = 1024
HEADS = 16
HD = 64
FF = 4096
LEN = 512
TOKENS = 32768


def levels(key, extent, shards, low, top_value):
    factor_of = 1.0
    for dim, parts in shards:
        draws = jax.random.uniform(jax.random.fold_in(jax.random.fold_in(key, 6), dim), (parts,), jnp.float32, low / len(shards), top_value / len(shards))
        factor_of = factor_of * jnp.repeat(jnp.exp(draws), extent[dim] // parts).reshape((-1,) + (1,) * (len(extent) - 1 - dim))
    return factor_of


def noise(stream_key, dims, deviation, most, shards=(), kind=jnp.bfloat16):
    factor_of = levels(stream_key, dims, shards, -0.22, 0.18) if shards else 1.0
    entries = jax.random.normal(stream_key, dims, jnp.float32) * deviation * factor_of
    return jnp.minimum(jnp.maximum(entries, -most), most).astype(kind)


def setup_inputs(seed: int = 0) -> dict:
    key_of = jax.random.split(jax.random.key(seed), 16)
    return {
        "tokens": noise(key_of[0], (TOKENS, D), 1.0, 6.0, ((0, 32),)),
        "cotangent": noise(key_of[1], (TOKENS, D), 1.0, 6.0, ((0, 32),)),
        "w_qkv": noise(key_of[2], (D, 3 * D), D ** -0.5, 0.1875, ((0, 32),)),
        "q_bias": noise(key_of[3], (D,), 0.3, 2.0, ((0, 32),)),
        "v_bias": noise(key_of[4], (D,), 0.3, 2.0, ((0, 32),)),
        "w_out": noise(key_of[5], (D, D), (D // 16) ** -0.5, 0.75, ((0, 32),)),
        "out_bias": noise(key_of[6], (D,), 0.3, 2.0, ((0, 32),)),
        "attn_gain": jnp.clip(1.0 + 0.1 * jax.random.normal(key_of[7], (D,), jnp.float32), 0.5, 1.5).astype(jnp.bfloat16),
        "attn_shift": noise(key_of[8], (D,), 0.3, 2.0, ((0, 32),)),
        "w_up": noise(key_of[9], (D, FF), D ** -0.5, 0.1875, ((0, 32),)),
        "up_bias": noise(key_of[10], (FF,), 0.3, 2.0, ((0, 32),)),
        "w_down": noise(key_of[11], (FF, D), (FF // 4) ** -0.5, 0.1875, ((0, 32),)),
        "down_bias": noise(key_of[12], (D,), 0.3, 2.0, ((0, 32),)),
        "mlp_gain": jnp.clip(1.0 + 0.1 * jax.random.normal(key_of[13], (D,), jnp.float32), 0.5, 1.5).astype(jnp.bfloat16),
        "mlp_shift": noise(key_of[14], (D,), 0.3, 2.0, ((0, 32),)),
    }


@jax.custom_vjp
def low(v):
    return lax.optimization_barrier(v.astype(jnp.bfloat16)).astype(jnp.float32)

@jax.custom_vjp
def low_back(v):
    return v

def low_keep(v):
    return (low(v), None)

def low_pass(kept, grad):
    return (grad,)

def back_keep(v):
    return (v, None)

def back_low(kept, grad):
    return (low(grad),)
low.defvjp(low_keep, low_pass)
low_back.defvjp(back_keep, back_low)

def layer_norm(value, gain, shift):
    center = value - lax.optimization_barrier(jnp.mean(value, axis=-1, keepdims=True))
    spread = lax.optimization_barrier(jnp.mean(center * center, axis=-1, keepdims=True))
    return center * lax.rsqrt(spread + 1e-05) * gain + shift

def matmul(left, right):
    return jnp.dot(left, right, precision=lax.Precision.HIGHEST)

def attend(triple):
    queries, keys_rows, values_rows = triple
    scale = 1.0 / math.sqrt(HD)
    queries = queries.reshape(LEN, HEADS, HD)
    keys_rows = keys_rows.reshape(LEN, HEADS, HD)
    values_rows = values_rows.reshape(LEN, HEADS, HD)
    scores = low_back(jnp.einsum('qhd,khd->hqk', queries, keys_rows, precision=lax.Precision.HIGHEST) * scale)
    probs = low(jax.nn.softmax(scores, axis=-1))
    context = jnp.einsum('hqk,khd->qhd', probs, values_rows, precision=lax.Precision.HIGHEST)
    return context.reshape(LEN, D)

def forward(inputs, w_qkv, q_bias, v_bias, w_out, out_bias, attn_gain, attn_shift, w_up, up_bias, w_down, down_bias, mlp_gain, mlp_shift):
    bias_full = jnp.concatenate([q_bias, jnp.zeros_like(q_bias), v_bias])
    projected = low(low_back(matmul(inputs, w_qkv) + bias_full))
    count = inputs.shape[0] // LEN
    queries = projected[:, :D].reshape(count, LEN, D)
    keys_rows = projected[:, D:2 * D].reshape(count, LEN, D)
    values_rows = projected[:, 2 * D:].reshape(count, LEN, D)
    context = lax.map(jax.checkpoint(attend), (queries, keys_rows, values_rows))
    context = low(low_back(context.reshape(count * LEN, D)))
    attn = low_back(matmul(context, w_out) + out_bias)
    normed = layer_norm(inputs + attn, attn_gain, attn_shift)
    upper = low_back(matmul(low(normed), w_up) + up_bias)
    active = low(jax.nn.gelu(upper, approximate=False))
    branch = low_back(matmul(active, w_down) + down_bias)
    return layer_norm(normed + branch, mlp_gain, mlp_shift)

def reference(tokens, cotangent, w_qkv, q_bias, v_bias, w_out, out_bias, attn_gain, attn_shift, w_up, up_bias, w_down, down_bias, mlp_gain, mlp_shift):
    params = tuple((p.astype(jnp.float32) for p in (w_qkv, q_bias, v_bias, w_out, out_bias, attn_gain, attn_shift, w_up, up_bias, w_down, down_bias, mlp_gain, mlp_shift)))
    groups = tokens.shape[0] // (8 * LEN)
    inputs = tokens.astype(jnp.float32).reshape(groups, 8 * LEN, D)
    cotan = cotangent.astype(jnp.float32).reshape(groups, 8 * LEN, D)

    def step(totals, pair):
        block_in, block_cot = pair
        result, pull = jax.vjp(forward, block_in, *params)
        grads = pull(block_cot)
        totals = tuple((a + b for a, b in zip(totals, grads[1:])))
        return (totals, (result.astype(jnp.bfloat16), grads[0].astype(jnp.bfloat16)))
    start = tuple((jnp.zeros(p.shape, jnp.float32) for p in params))
    totals, (outs, dins) = lax.scan(step, start, (inputs, cotan))
    return (outs.reshape(-1, D), dins.reshape(-1, D)) + totals
```

```python
import functools
import math

import jax
import jax.numpy as jnp
from jax import lax
from jax.experimental import pallas as pl
from jax.experimental.pallas import tpu as pltpu
from jax.sharding import PartitionSpec as P

HD = 64
LEN = 512
EPS = 1e-05
CHUNKS = 32
F32 = jnp.float32
BF16 = jnp.bfloat16
MIB = 1 << 20


def params(limit=48):
    return pltpu.CompilerParams(vmem_limit_bytes=limit * MIB)


COST = 0.02


def cost(flops, nbytes, trans=0):
    return pl.CostEstimate(
        flops=int(COST * flops), bytes_accessed=int(COST * nbytes), transcendentals=int(COST * trans)
    )


def dot(a, b):
    return jnp.dot(a, b, preferred_element_type=F32)


def dot_t(a, b):
    return lax.dot_general(a, b, (((1,), (1,)), ((), ())), preferred_element_type=F32)


def t_dot(a, b):
    return lax.dot_general(a, b, (((0,), (0,)), ((), ())), preferred_element_type=F32)


SCALAR = pl.BlockSpec(memory_space=pltpu.SMEM)


def row_spec(block, width):
    return pl.BlockSpec((block, width), lambda i: (i, 0))


def full_spec(shape):
    return pl.BlockSpec(shape, lambda i: (0,) * len(shape))


def project_kernel(me_ref, x_ref, *refs):
    pieces, (o_ref, w_ref, t_ref, sems) = refs[:4], refs[4:]
    j = pl.program_id(0)
    block = o_ref.shape[1]
    width = x_ref.shape[1]
    size = width // CHUNKS

    @pl.when(j == 0)
    def _():
        cut = pieces[0].shape[2]
        copies = []
        for which, piece in enumerate(pieces):
            right, core = which % 2, which // 2
            for k in range(piece.shape[0]):
                a, b, z = k >> 3, (k >> 2) & 1, k & 3
                mask = core | (a << 1 | b << 2 if right else a << 2 | b << 1) | z << 3
                at = pl.multiple_of(jnp.bitwise_xor(me_ref[0], mask) * size, size)
                cols = pl.ds(cut, piece.shape[2]) if right else pl.ds(0, cut)
                copies.append(
                    pltpu.make_async_copy(
                        piece.at[k], w_ref.at[pl.ds(at, size), cols], sems.at[len(copies)]
                    )
                )
        for copy in copies:
            copy.start()
        for copy in copies:
            copy.wait()
        table = w_ref[:, 3 * width :].astype(F32).T
        t_ref[...] = table[: t_ref.shape[0]]

    per = width // block
    at = pl.multiple_of((j % per) * block, block)
    bias = jnp.where(
        j < per,
        t_ref[0:1, pl.ds(at, block)],
        jnp.where(j >= 2 * per, t_ref[1:2, pl.ds(at, block)], 0.0),
    )
    w = w_ref[:, pl.ds(pl.multiple_of(j * block, block), block)]
    o_ref[...] = (dot(x_ref[...], w) + bias).astype(BF16)


def project(me, x, pieces, block=512):
    rows, width = x.shape
    cols = 3 * width
    held = pieces[0].shape[2] + pieces[1].shape[2]
    return pl.pallas_call(
        project_kernel,
        grid=(cols // block,),
        in_specs=[SCALAR, full_spec((rows, width))] + [pl.BlockSpec(memory_space=pl.ANY)] * 4,
        out_specs=[
            pl.BlockSpec((rows, block), lambda j: (0, j)),
            full_spec((width, held)),
            full_spec((16, width)),
        ],
        out_shape=[
            jax.ShapeDtypeStruct((rows, cols), BF16),
            jax.ShapeDtypeStruct((width, held), BF16),
            jax.ShapeDtypeStruct((16, width), F32),
        ],
        scratch_shapes=[pltpu.SemaphoreType.DMA((2 * CHUNKS,))],
        compiler_params=params(),
        cost_estimate=cost(2 * rows * width * cols, 2 * (rows * width + 2 * width * cols + rows * cols)),
        name="project",
    )(me, x, *pieces)


def head_mask(shape, h):
    lane = lax.broadcasted_iota(jnp.int32, shape, 1)
    return (lane >= h * HD) & (lane < (h + 1) * HD)


def attend_kernel(q_ref, k_ref, v_ref, ctx_ref, lse_ref):
    q = q_ref[...] * jnp.asarray(1.0 / math.sqrt(HD), BF16)
    k = k_ref[...]
    vt = v_ref[...].T
    parts = []
    for h in range(2):
        qh = jnp.where(head_mask(q.shape, h), q, jnp.zeros_like(q))
        s = dot_t(k, qh)
        m = jnp.max(s, axis=0, keepdims=True)
        e = jnp.exp(s - m)
        total = jnp.sum(e, axis=0, keepdims=True)
        c = dot(vt[h * HD : (h + 1) * HD, :], e.astype(BF16))
        parts.append(c * (1.0 / total))
        lse_ref[0, 0, h : h + 1, :] = m + jnp.log(total)
    ctx_ref[...] = jnp.concatenate(parts, axis=0).T.astype(BF16)


def attend(qkv, width):
    rows = qkv.shape[0]
    count, pairs = rows // LEN, width // 128
    return pl.pallas_call(
        attend_kernel,
        grid=(pairs, count),
        in_specs=[
            pl.BlockSpec((LEN, 128), lambda p, s: (s, p)),
            pl.BlockSpec((LEN, 128), lambda p, s: (s, pairs + p)),
            pl.BlockSpec((LEN, 128), lambda p, s: (s, 2 * pairs + p)),
        ],
        out_specs=[
            pl.BlockSpec((LEN, 128), lambda p, s: (s, p)),
            pl.BlockSpec((1, 1, 2, LEN), lambda p, s: (p, s, 0, 0)),
        ],
        out_shape=[
            jax.ShapeDtypeStruct((rows, width), BF16),
            jax.ShapeDtypeStruct((pairs, count, 2, LEN), F32),
        ],
        compiler_params=params(),
        cost_estimate=cost(
            rows * width * LEN * 4 * 4, 8 * rows * width, rows * width * LEN // HD
        ),
        name="attend",
    )(qkv, qkv, qkv)


def attend_back_kernel(q_ref, k_ref, v_ref, c_ref, d_ref, lse_ref, dp_ref, sq_ref, sv_ref):
    scale = 1.0 / math.sqrt(HD)
    q = q_ref[...] * jnp.asarray(scale, BF16)
    k = k_ref[...]
    v = v_ref[...]
    d = d_ref[...]
    kt = k.T
    prod = (d.astype(F32) * c_ref[...].astype(F32)).T
    dk = dv = None
    parts = []
    for h in range(2):
        mask = head_mask(q.shape, h)
        qh = jnp.where(mask, q, jnp.zeros_like(q))
        dh = jnp.where(mask, d, jnp.zeros_like(d))
        delta = jnp.sum(prod[h * HD : (h + 1) * HD, :], axis=0, keepdims=True)
        p = jnp.exp(dot_t(k, qh) - lse_ref[0, 0, h : h + 1, :])
        ds = (p * (dot_t(v, dh) - delta)).astype(BF16)
        dv_h = dot(p.astype(BF16), dh)
        dk_h = dot(ds, qh)
        dv = dv_h if dv is None else dv + dv_h
        dk = dk_h if dk is None else dk + dk_h
        parts.append(dot(kt[h * HD : (h + 1) * HD, :], ds) * scale)
    dq = jnp.concatenate(parts, axis=0).T.astype(BF16)
    dv = dv.astype(BF16)
    dp_ref[:, 0:128] = dq
    dp_ref[:, 128:256] = dk.astype(BF16)
    dp_ref[:, 256:384] = dv
    sq = jnp.sum(dq.astype(F32), axis=0, keepdims=True)
    sv = jnp.sum(dv.astype(F32), axis=0, keepdims=True)
    first = pl.program_id(1) == 0

    @pl.when(first)
    def _():
        sq_ref[...] = sq
        sv_ref[...] = sv

    @pl.when(jnp.logical_not(first))
    def _():
        sq_ref[...] += sq
        sv_ref[...] += sv


def attend_back(qkv, ctx, dctx, lse, width, start, n_pairs):
    rows = qkv.shape[0]
    count, pairs = rows // LEN, width // 128
    cols = n_pairs * 128
    sum_block = pl.BlockSpec((1, 128), lambda p, s: (0, p))
    return pl.pallas_call(
        attend_back_kernel,
        grid=(n_pairs, count),
        in_specs=[
            pl.BlockSpec((LEN, 128), lambda p, s: (s, start + p)),
            pl.BlockSpec((LEN, 128), lambda p, s: (s, pairs + start + p)),
            pl.BlockSpec((LEN, 128), lambda p, s: (s, 2 * pairs + start + p)),
            pl.BlockSpec((LEN, 128), lambda p, s: (s, start + p)),
            pl.BlockSpec((LEN, 128), lambda p, s: (s, start + p)),
            pl.BlockSpec((1, 1, 2, LEN), lambda p, s: (start + p, s, 0, 0)),
        ],
        out_specs=[pl.BlockSpec((LEN, 384), lambda p, s: (s, p)), sum_block, sum_block],
        out_shape=[jax.ShapeDtypeStruct((rows, 3 * cols), BF16)]
        + [jax.ShapeDtypeStruct((1, cols), F32)] * 2,
        compiler_params=params(),
        cost_estimate=cost(rows * cols * LEN * 10 * 4, 16 * rows * cols, rows * cols * LEN // HD),
        name="attend_back",
    )(qkv, qkv, qkv, ctx, dctx, lse)


def out_weight(held):
    _, rows, width = held.shape
    size = width // CHUNKS
    return pl.BlockSpec((CHUNKS, size, width), lambda i: (0, rows // size - 1, 0))


def deep_weight(held, which):
    _, rows, width = held.shape
    return pl.BlockSpec((CHUNKS, (rows - width // CHUNKS) // 2, width), lambda i: (0, which, 0))


def out_norm_kernel(c_ref, w_ref, b_ref, x_ref, g_ref, s_ref, hat_ref, rstd_ref, low_ref):
    w = w_ref[...].reshape(-1, x_ref.shape[1])
    h = x_ref[...].astype(F32) + (dot(c_ref[...], w) + b_ref[...])
    center = h - jnp.mean(h, axis=-1, keepdims=True)
    rstd = lax.rsqrt(jnp.mean(center * center, axis=-1, keepdims=True) + EPS)
    hat = center * rstd
    hat_ref[...] = hat
    rstd_ref[...] = rstd
    low_ref[...] = (hat * g_ref[...] + s_ref[...]).astype(BF16)


def out_norm(ctx, held, bias, tokens, gain, shift, block=256):
    rows, width = tokens.shape
    vec = full_spec((1, width))
    return pl.pallas_call(
        out_norm_kernel,
        grid=(rows // block,),
        in_specs=[
            row_spec(block, width),
            out_weight(held),
            vec,
            row_spec(block, width),
            vec,
            vec,
        ],
        out_specs=[row_spec(block, width), row_spec(block, 1), row_spec(block, width)],
        out_shape=[
            jax.ShapeDtypeStruct((rows, width), F32),
            jax.ShapeDtypeStruct((rows, 1), F32),
            jax.ShapeDtypeStruct((rows, width), BF16),
        ],
        compiler_params=params(),
        cost_estimate=cost(2 * rows * width * width, 14 * rows * width),
        name="out_norm",
    )(ctx, held, bias, tokens, gain, shift)


ERF_P = 0.3275911 / math.sqrt(2.0)
ERF_A = (0.254829592, -0.284496736, 1.421413741, -1.453152027, 1.061405429)


def gelu_pair(u):
    t = 1.0 / (1.0 + ERF_P * jnp.abs(u))
    e = jnp.exp(-0.5 * (u * u))
    poly = t * (ERF_A[0] + t * (ERF_A[1] + t * (ERF_A[2] + t * (ERF_A[3] + t * ERF_A[4]))))
    tail = 0.5 * poly * e
    cdf = jnp.where(u >= 0, 1.0 - tail, tail)
    return u * cdf, cdf + u * e * (1.0 / math.sqrt(2.0 * math.pi))


def up_kernel(x_ref, w_ref, b_ref, act_ref, slope_ref):
    block = act_ref.shape[1]
    u = dot(x_ref[...], w_ref[...].reshape(-1, block)) + b_ref[...]
    act, slope = gelu_pair(u)
    act_ref[...] = act.astype(BF16)
    slope_ref[...] = slope.astype(BF16)


def up_gelu(x, held, bias, block=512):
    rows, width = x.shape
    cols = bias.shape[1]
    per = width // block
    col = pl.BlockSpec((rows, block), lambda j: (0, j))
    return pl.pallas_call(
        up_kernel,
        grid=(cols // block,),
        in_specs=[
            full_spec((rows, width)),
            pl.BlockSpec((CHUNKS, width // CHUNKS, block), lambda j: (0, j // per, j % per)),
            pl.BlockSpec((1, block), lambda j: (0, j)),
        ],
        out_specs=[col, col],
        out_shape=[jax.ShapeDtypeStruct((rows, cols), BF16)] * 2,
        compiler_params=params(),
        cost_estimate=cost(
            2 * rows * width * cols, 2 * (width * cols + 2 * rows * cols), 2 * rows * cols
        ),
        name="up_gelu",
    )(x, held, bias)


def down_norm_kernel(
    a_ref, w_ref, b_ref, hat1_ref, g1_ref, s1_ref, g2_ref, s2_ref, cot_ref,
    out_ref, dh_ref, dm_ref, dg_ref, ds_ref, db_ref,
):
    n1 = hat1_ref[...] * g1_ref[...] + s1_ref[...]
    h = n1 + (dot(a_ref[...], w_ref[...].reshape(-1, n1.shape[1])) + b_ref[...])
    center = h - jnp.mean(h, axis=-1, keepdims=True)
    rstd = lax.rsqrt(jnp.mean(center * center, axis=-1, keepdims=True) + EPS)
    hat = center * rstd
    out_ref[...] = (hat * g2_ref[...] + s2_ref[...]).astype(BF16)
    cot = cot_ref[...].astype(F32)
    wide = cot * g2_ref[...]
    mean_a = jnp.mean(wide, axis=-1, keepdims=True)
    mean_b = jnp.mean(wide * hat, axis=-1, keepdims=True)
    dh = rstd * (wide - mean_a - hat * mean_b)
    dh_ref[...] = dh
    dm = dh.astype(BF16)
    dm_ref[...] = dm

    @pl.when(pl.program_id(0) == 0)
    def _():
        dg_ref[...] = jnp.zeros_like(dg_ref)
        ds_ref[...] = jnp.zeros_like(ds_ref)
        db_ref[...] = jnp.zeros_like(db_ref)

    dg_ref[...] += jnp.sum(cot * hat, axis=0, keepdims=True)
    ds_ref[...] += jnp.sum(cot, axis=0, keepdims=True)
    db_ref[...] += jnp.sum(dm.astype(F32), axis=0, keepdims=True)


def down_norm(act, held, bias, hat1, g1, s1, g2, s2, cot, block=256):
    rows, width = hat1.shape
    deep = act.shape[1]
    vec = full_spec((1, width))
    row = row_spec(block, width)
    return pl.pallas_call(
        down_norm_kernel,
        grid=(rows // block,),
        in_specs=[row_spec(block, deep), deep_weight(held, 1), vec, row, vec, vec, vec, vec, row],
        out_specs=[row, row, row, vec, vec, vec],
        out_shape=[
            jax.ShapeDtypeStruct((rows, width), BF16),
            jax.ShapeDtypeStruct((rows, width), F32),
            jax.ShapeDtypeStruct((rows, width), BF16),
        ]
        + [jax.ShapeDtypeStruct((1, width), F32)] * 3,
        compiler_params=params(),
        cost_estimate=cost(2 * rows * width * deep, 2 * deep * (rows + width) + 14 * rows * width),
        name="down_norm",
    )(act, held, bias, hat1, g1, s1, g2, s2, cot)


def split(value, core, chunk, keep_ref, send_ref):
    value = value.astype(BF16).reshape(-1, 2, 2, chunk // 2, value.shape[1])
    for half in range(2):
        even = value[:, 0, half].reshape(keep_ref.shape[1:])
        odd = value[:, 1, half].reshape(keep_ref.shape[1:])
        keep_ref[half] = jnp.where(core == 0, even, odd)
        send_ref[half] = jnp.where(core == 0, odd, even)


def join(keep, send, chunk):
    cols = keep.shape[-1]
    pair = [v.reshape(2, -1, chunk // 2, cols) for v in (keep, send)]
    return jnp.stack(pair, axis=0).transpose(2, 0, 1, 3, 4).reshape(-1, cols)


def down_grad_kernel(core_ref, a_ref, b_ref, keep_ref, send_ref):
    chunk = keep_ref.shape[1]
    split(t_dot(a_ref[...], b_ref[...]), core_ref[0], chunk, keep_ref, send_ref)


def down_grad(core, a, b):
    rows, deep = a.shape
    cols = b.shape[1]
    block = 4 * deep // CHUNKS
    out = pl.BlockSpec((2, block // 4, cols), lambda j: (0, j, 0))
    return pl.pallas_call(
        down_grad_kernel,
        grid=(deep // block,),
        in_specs=[SCALAR, pl.BlockSpec((rows, block), lambda j: (0, j)), full_spec((rows, cols))],
        out_specs=[out, out],
        out_shape=[jax.ShapeDtypeStruct((2, deep // 4, cols), BF16)] * 2,
        compiler_params=params(),
        cost_estimate=cost(2 * rows * deep * cols, 2 * (rows * deep + rows * cols + deep * cols)),
        name="down_grad",
    )(core, a, b)


def attn_grad_kernel(core_ref, xt_ref, *refs, n_parts, more):
    parts, rest = refs[:n_parts], refs[n_parts:]
    keep_ref, send_ref = rest[-2:]
    chunk = 32
    at = 0

    def put(value):
        nonlocal at
        cols = value.shape[1]
        here = [ref.at[:, :, at : at + cols] for ref in (keep_ref, send_ref)]
        split(value, core_ref[0], chunk, *here)
        at += cols

    for ref in parts:
        put(dot(xt_ref[...], ref[...]))
    if more == "out":
        put(t_dot(rest[0][...], rest[1][...]))
    else:
        put(rest[0][...])


def attn_grad(core, xt, parts, extra, more, block=256):
    width, rows = xt.shape
    in_specs = [SCALAR, row_spec(block, rows)] + [full_spec(p.shape) for p in parts]
    cols = sum(p.shape[1] for p in parts)
    if more == "out":
        in_specs += [pl.BlockSpec((rows, block), lambda i: (0, i)), full_spec(extra[1].shape)]
        cols += extra[1].shape[1]
    else:
        in_specs += [row_spec(block, extra[0].shape[1])]
        cols += extra[0].shape[1]
    out = pl.BlockSpec((2, block // 4, cols), lambda i: (0, i, 0))
    return pl.pallas_call(
        functools.partial(attn_grad_kernel, n_parts=len(parts), more=more),
        grid=(width // block,),
        in_specs=in_specs,
        out_specs=[out, out],
        out_shape=[jax.ShapeDtypeStruct((2, width // 4, cols), BF16)] * 2,
        compiler_params=params(),
        cost_estimate=cost(2 * rows * width * cols, 2 * (rows * width + cols * (rows + width))),
        name="attn_grad",
    )(core, xt, *parts, *extra)


def up_back_kernel(
    core_ref, dm_ref, w_ref, slope_ref, x_ref, du_ref, keep_ref, send_ref, db_ref, xt_ref
):
    @pl.when(pl.program_id(0) == 0)
    def _():
        xt_ref[...] = x_ref[...].T

    w = w_ref[...].reshape(-1, dm_ref.shape[1])
    du = (dot_t(dm_ref[...], w) * slope_ref[...].astype(F32)).astype(BF16)
    du_ref[...] = du
    db_ref[...] = jnp.sum(du.astype(F32), axis=0, keepdims=True)
    split(dot(xt_ref[...], du), core_ref[0], xt_ref.shape[0] // CHUNKS, keep_ref, send_ref)


def up_back(core, dm, held, slope, x):
    rows, width = dm.shape
    deep = slope.shape[1]
    block = 4 * deep // CHUNKS
    col = pl.BlockSpec((rows, block), lambda j: (0, j))
    half = pl.BlockSpec((2, width // 4, block), lambda j: (0, 0, j))
    return pl.pallas_call(
        up_back_kernel,
        grid=(deep // block,),
        in_specs=[
            SCALAR,
            full_spec((rows, width)),
            pl.BlockSpec((4, deep // CHUNKS, width), lambda j: (j, 1, 0)),
            col,
            full_spec((rows, width)),
        ],
        out_specs=[col, half, half, pl.BlockSpec((1, block), lambda j: (0, j))],
        out_shape=[
            jax.ShapeDtypeStruct((rows, deep), BF16),
            jax.ShapeDtypeStruct((2, width // 4, deep), BF16),
            jax.ShapeDtypeStruct((2, width // 4, deep), BF16),
            jax.ShapeDtypeStruct((1, deep), F32),
        ],
        scratch_shapes=[pltpu.VMEM((width, rows), BF16)],
        compiler_params=params(),
        cost_estimate=cost(4 * rows * width * deep, 4 * deep * (rows + width) + 4 * rows * width),
        name="up_back",
    )(core, dm, held, slope, x)


def norm_back_kernel(
    du_ref, w_ref, dh2_ref, hat_ref, rstd_ref, g_ref, dh_ref, da_ref, dg_ref, ds_ref, db_ref
):
    width = dh2_ref.shape[1]
    dn = dh2_ref[...]
    size = width // CHUNKS
    for j in range(du_ref.shape[1] // width):
        w = w_ref[:, j * size : (j + 1) * size, :].reshape(width, width)
        dn = dn + dot_t(du_ref[:, j * width : (j + 1) * width], w)
    hat = hat_ref[...]
    wide = dn * g_ref[...]
    mean_a = jnp.mean(wide, axis=-1, keepdims=True)
    mean_b = jnp.mean(wide * hat, axis=-1, keepdims=True)
    dh = rstd_ref[...] * (wide - mean_a - hat * mean_b)
    dh_ref[...] = dh
    da = dh.astype(BF16)
    da_ref[...] = da

    @pl.when(pl.program_id(0) == 0)
    def _():
        dg_ref[...] = jnp.zeros_like(dg_ref)
        ds_ref[...] = jnp.zeros_like(ds_ref)
        db_ref[...] = jnp.zeros_like(db_ref)

    dg_ref[...] += jnp.sum(dn * hat, axis=0, keepdims=True)
    ds_ref[...] += jnp.sum(dn, axis=0, keepdims=True)
    db_ref[...] += jnp.sum(da.astype(F32), axis=0, keepdims=True)


def norm_back(du, held, dh2, hat, rstd, gain, block=256):
    rows, width = hat.shape
    deep = du.shape[1]
    vec = full_spec((1, width))
    row = row_spec(block, width)
    return pl.pallas_call(
        norm_back_kernel,
        grid=(rows // block,),
        in_specs=[row_spec(block, deep), deep_weight(held, 0), row, row, row_spec(block, 1), vec],
        out_specs=[row, row, vec, vec, vec],
        out_shape=[
            jax.ShapeDtypeStruct((rows, width), F32),
            jax.ShapeDtypeStruct((rows, width), BF16),
        ]
        + [jax.ShapeDtypeStruct((1, width), F32)] * 3,
        compiler_params=params(),
        cost_estimate=cost(2 * rows * width * deep, 2 * deep * (rows + width) + 14 * rows * width),
        name="norm_back",
    )(du, held, dh2, hat, rstd, gain)


def context_back_kernel(da_ref, w_ref, o_ref):
    o_ref[...] = dot_t(da_ref[...], w_ref[...].reshape(-1, da_ref.shape[1])).astype(BF16)


def context_back(da, held, block=512):
    rows, width = da.shape
    return pl.pallas_call(
        context_back_kernel,
        grid=(rows // block,),
        in_specs=[row_spec(block, width), out_weight(held)],
        out_specs=row_spec(block, width),
        out_shape=jax.ShapeDtypeStruct((rows, width), BF16),
        compiler_params=params(),
        cost_estimate=cost(2 * rows * width * width, 6 * rows * width),
        name="context_back",
    )(da, held)


def input_back_kernel(*refs):
    *parts, w_ref, dh_ref, o_ref = refs
    width = o_ref.shape[1]
    total = dh_ref[...]
    for which in range(3):
        pieces = [
            ref[:, at : at + 128]
            for ref in parts
            for at in range(which * 128, ref.shape[1], 384)
        ]
        col = which * width
        total = total + dot_t(jnp.concatenate(pieces, axis=1), w_ref[:, col : col + width])
    o_ref[...] = total.astype(BF16)


def input_back(parts, w, dh, block=256):
    rows, width = dh.shape
    return pl.pallas_call(
        input_back_kernel,
        grid=(rows // block,),
        in_specs=[row_spec(block, p.shape[1]) for p in parts]
        + [pl.BlockSpec((width, 3 * width), lambda i: (0, 0)), row_spec(block, width)],
        out_specs=row_spec(block, width),
        out_shape=jax.ShapeDtypeStruct((rows, width), BF16),
        compiler_params=params(),
        cost_estimate=cost(6 * rows * width * width, 18 * rows * width),
        name="input_back",
    )(*parts, w, dh)


def exchange(x, n, mask):
    return lax.ppermute(x, "dp", [(i, i ^ mask) for i in range(n)])


def pick(x, axis, index):
    return lax.dynamic_index_in_dim(x, index, axis, keepdims=False)


def tie(*values):
    return lax.optimization_barrier(values)


class Scatter:
    def __init__(self, keep, send, n, r):
        self.n, self.h, self.me, self.cols = n, r // 2, lax.axis_index("dp"), keep.shape[-1]
        self.held = [(keep, exchange(send, n, 1))] * 2
        self.left = [[4, 3, 2, 1], [4, 3, 2, 1]]
        self.step = 0

    def part(self, side, bit, which):
        left = self.left[side]
        at, size = left.index(bit), 1 << len(left)
        shape = (1 << at, 2, size >> (at + 1), self.h, self.cols)
        total = None
        for value in self.held[side]:
            lead = value.size // math.prod(shape)
            value = value.reshape(lead, *shape)
            start = (side if lead == 2 else 0, 0, which, 0, 0, 0)
            value = lax.dynamic_slice(value, start, (1, shape[0], 1, *shape[2:])).astype(F32)
            total = value if total is None else total + value
        return total.reshape(size // 2, self.h, self.cols)

    def behind(self, along):
        pairs = list(self.held)
        flat = tie(*pairs[0], *pairs[1], *along)
        self.held = [flat[:2], flat[2:4]]
        return flat[4:]

    def halve(self, *along):
        along = self.behind(along)
        bits = ((2, 1), (1, 2))
        sums = []
        for side in range(2):
            bit = bits[side][self.step]
            mine = (self.me >> bit) & 1
            sums += [self.part(side, bit, which).astype(BF16) for which in (1 - mine, mine)]
        *sums, = tie(*sums, *along)
        sums, along = sums[:4], sums[4:]
        for side in range(2):
            bit = bits[side][self.step]
            self.held[side] = (sums[2 * side + 1], exchange(sums[2 * side], self.n, 1 << bit))
            self.left[side].remove(bit)
        self.step += 1
        return along[0] if len(along) == 1 else along

    def column_one(self, *along):
        along = self.behind(along)
        mine = self.me >> 4
        sent, kept = [
            jnp.concatenate([self.part(side, 4, which) for side in range(2)], axis=1).astype(BF16)
            for which in (1 - mine, mine)
        ]
        sent, kept, *along = tie(sent, kept, *along)
        self.pair = (kept, exchange(sent, self.n, 16))
        return along[0] if len(along) == 1 else along

    def column_two(self, *along):
        *self.pair, = tie(*self.pair, *along)
        self.pair, along = self.pair[:2], self.pair[2:]
        mine = (self.me >> 3) & 1
        sent, kept = [
            sum(pick(value, 0, which).astype(F32) for value in self.pair) for which in (1 - mine, mine)
        ]
        sent, kept, *along = tie(sent.astype(BF16), kept, *along)
        self.last = [kept, exchange(sent, self.n, 8)]
        return along[0] if len(along) == 1 else along

    def column(self, *along):
        along = self.behind(along)
        mine = self.me >> 3
        sums = [
            jnp.concatenate(
                [
                    sum(pick(v, 0, mine ^ k).astype(F32) for v in self.held[side])
                    for side in range(2)
                ],
                axis=0,
            )
            for k in range(4)
        ]
        *sums, = tie(sums[0], *[v.astype(BF16) for v in sums[1:]], *along)
        sums, along = sums[:4], sums[4:]
        self.last = sums[:1] + [exchange(sums[k], self.n, k << 3) for k in (1, 2, 3)]
        return along[0] if len(along) == 1 else along

    def result(self):
        return sum(value.astype(F32) for value in self.last)


class PlainScatter:
    def __init__(self, keep, send, n, r):
        whole = join(keep, send, keep.shape[1] * 4 // CHUNKS)
        self.total = lax.psum_scatter(whole.astype(F32), "dp", scatter_dimension=0, tiled=True)

    def halve(self, *along):
        return along[0] if len(along) == 1 else along

    column = column_one = column_two = halve

    def result(self):
        return self.total


def gather(x):
    return lax.all_gather(x, "dp", axis=0, tiled=True)


def gather_pieces(x, n):
    cut = x.shape[1] // 256 * 128
    near = [x] + [exchange(x, n, k << 3) for k in (1, 2, 3)]
    sides = []
    for low, high, bits in ((0, cut, (1, 2)), (cut, x.shape[1], (2, 1))):
        side = jnp.concatenate([v[:, low:high] for v in near], axis=0)
        sides.append((side, bits))
    for step in range(2):
        sides = [
            (jnp.concatenate([v, exchange(v, n, 1 << bits[step])], axis=0), bits) for v, bits in sides
        ]
    mine = [v for v, _ in sides]
    pieces = mine + [exchange(v, n, 1) for v in mine]
    return [v.reshape(-1, *x.shape[:1], v.shape[1]) for v in pieces]


def plain_pieces(whole):
    cut = whole.shape[1] // 256 * 128
    chips = whole.reshape(4, 2, 2, 2, -1, whole.shape[1])
    left = chips[..., :cut].transpose(3, 1, 2, 0, 4, 5)
    right = chips[..., cut:].transpose(3, 2, 1, 0, 4, 5)
    return [v[core].reshape(16, -1, v.shape[-1]) for core in range(2) for v in (left, right)]


def columns(vector, r):
    return vector.reshape(-1, r).T


def table_of(vectors, n, r):
    parts = [v.reshape(n, -1, r).transpose(0, 2, 1).reshape(n * r, -1) for v in vectors]
    return jnp.concatenate(parts, axis=1)


def local(
    n,
    tokens,
    cotangent,
    w_qkv,
    q_bias,
    v_bias,
    w_out,
    out_bias,
    attn_gain,
    attn_shift,
    w_up,
    up_bias,
    w_down,
    down_bias,
    mlp_gain,
    mlp_shift,
):
    rows, width = tokens.shape
    r = w_qkv.shape[0]
    wide = w_up.shape[1] // width
    vectors = (
        q_bias, v_bias, out_bias, attn_gain, attn_shift, down_bias, mlp_gain, mlp_shift, up_bias,
    )
    small = jnp.concatenate([columns(v, r) for v in vectors], axis=1)
    small = jnp.pad(small, ((0, 0), (0, 128 - small.shape[1])))
    first = jnp.concatenate([w_qkv, small], axis=1)
    if n == CHUNKS:
        blocks = [w_up[:, j * width : (j + 1) * width] for j in range(wide)]
        held = gather(jnp.concatenate(blocks + [w_down, w_out], axis=0))
        held = held.reshape(CHUNKS, -1, width)
        pieces = gather_pieces(first, n)
        scatter, me = Scatter, lax.axis_index("dp")
    else:
        up = gather(w_up).reshape(CHUNKS, width // CHUNKS, wide, width).transpose(0, 2, 1, 3)
        up = up.reshape(CHUNKS, wide * width // CHUNKS, width)
        down = gather(w_down).reshape(CHUNKS, wide * width // CHUNKS, width)
        out = gather(w_out).reshape(CHUNKS, width // CHUNKS, width)
        held = jnp.concatenate([up, down, out], axis=1)
        pieces = plain_pieces(gather(first))
        scatter, me = PlainScatter, jnp.int32(0)
    core = (me & 1).reshape(1)
    me = me.reshape(1)
    tokens_t, *pieces = tie(tokens.T, *pieces)

    qkv, w_full, table = project(me, tokens, pieces)
    ob, g1, s1, db, g2, s2 = [table[j : j + 1] for j in range(2, 8)]
    ub = table[8 : 8 + wide].reshape(wide, CHUNKS, -1).transpose(1, 0, 2).reshape(1, -1)

    ctx, lse = attend(qkv, width)
    hat1, rstd1, n1_low = out_norm(ctx, held, ob, tokens, g1, s1)
    act, slope = up_gelu(n1_low, held, ub)
    layer_out, dh2, dm, d_g2, d_s2, d_db = down_norm(
        act, held, db, hat1, g1, s1, g2, s2, cotangent
    )

    down_sum = scatter(*down_grad(core, act, dm), n, w_down.shape[0])
    du, up_keep, up_send, d_ub = up_back(core, dm, held, slope, n1_low)
    up_sum = scatter(up_keep, up_send, n, r)
    du = down_sum.halve(du)
    dh1, da, d_g1, d_s1, d_ob = norm_back(du, held, dh2, hat1, rstd1, g1)
    dctx = context_back(da, held)
    dctx = down_sum.halve(dctx)
    dctx = up_sum.halve(dctx)
    pairs = width // 128

    def back(start, count):
        return attend_back(qkv, ctx, dctx, lse, width, start, count)

    first, sq0, sv0 = back(0, 3)
    first = down_sum.column_one(first)
    keep, send = attn_grad(core, tokens_t, [first], [ctx, da], "out")
    keep, dctx = up_sum.halve(keep, dctx)
    early_sum = scatter(keep, send, n, r)
    second, sq1, sv1 = back(3, 3)
    second, dctx = down_sum.column_two(second, dctx)
    second, dctx = up_sum.column_one(second, dctx)
    second, dctx = early_sum.halve(second, dctx)
    third, sq2, sv2 = back(6, pairs - 6)
    third = early_sum.halve(third)
    third = up_sum.column_two(third)
    d_qb = jnp.concatenate([sq0, sq1, sq2], axis=1)
    d_vb = jnp.concatenate([sv0, sv1, sv2], axis=1)
    d_small = table_of([d_qb, d_vb, d_ob, d_g1, d_s1, d_db, d_g2, d_s2, d_ub], CHUNKS, width // CHUNKS)
    d_small = jnp.pad(d_small, ((0, 0), (0, 128 - d_small.shape[1]))).astype(BF16)
    keep, send = attn_grad(core, tokens_t, [second, third], [d_small], "small")
    late_sum = scatter(keep, send, n, r)
    dh1 = late_sum.halve(dh1)
    input_grad = input_back([first, second, third], w_full, dh1)
    input_grad = late_sum.halve(input_grad)
    input_grad = early_sum.column(input_grad)
    late_sum.column()

    early, late = early_sum.result(), late_sum.result()
    qkv_cols = 3 * 384
    d_qkv = jnp.concatenate([early[:, :qkv_cols], late[:, : 3 * width - qkv_cols]], axis=1)
    d_qkv = d_qkv.reshape(r, pairs, 3, 128).transpose(0, 2, 1, 3).reshape(r, 3 * width)
    d_out = early[:, qkv_cols:]
    d_small = late[:, 3 * width - qkv_cols :]

    def vector(start, k=1):
        return d_small[:, start : start + k].T.reshape(-1)

    d_qb, d_vb, d_ob, d_g1, d_s1, d_db, d_g2, d_s2 = [vector(j) for j in range(8)]
    d_ub = d_small[:, 8 : 8 + wide]
    d_ub = d_ub.T.reshape(-1)
    return (
        layer_out, input_grad, d_qkv, d_qb, d_vb, d_out, d_ob, d_g1, d_s1,
        up_sum.result(), d_ub, down_sum.result(), d_db, d_g2, d_s2,
    )


def solution(mesh):
    flat, square = P("dp"), P("dp", None)
    in_specs = (
        square, square, square, flat, flat, square, flat, flat, flat,
        square, flat, square, flat, flat, flat,
    )
    return jax.shard_map(
        functools.partial(local, mesh.shape["dp"]),
        mesh=mesh,
        in_specs=in_specs,
        out_specs=in_specs,
        check_vma=False,
    )
```

```python
import functools
import math

import jax
import jax.numpy as jnp
from jax import lax
from jax.experimental import pallas as pl
from jax.experimental.pallas import tpu as pltpu
from jax.sharding import PartitionSpec as P

HD = 64
LEN = 512
EPS = 1e-05
CHUNKS = 32
F32 = jnp.float32
BF16 = jnp.bfloat16
MIB = 1 << 20


def params(limit=48):
    return pltpu.CompilerParams(vmem_limit_bytes=limit * MIB)


COST = 0.02
PARTS = (3, 3, 2)
PLAN = {
    "up_back": [("D", "halve")],
    "norm_back": [("D", "halve"), ("U", "halve")],
    "first": [],
    "early": [("D", "column"), ("U", "halve")],
    "second": [("E", "halve")],
    "third": [("D", "after"), ("U", "column"), ("E", "halve")],
    "late": [("L", "halve")],
    "input_back": [("L", "halve"), ("U", "after"), ("E", "column"), ("L", "column")],
}


def cost(flops, nbytes, trans=0):
    return pl.CostEstimate(
        flops=int(COST * flops), bytes_accessed=int(COST * nbytes), transcendentals=int(COST * trans)
    )


def dot(a, b):
    return jnp.dot(a, b, preferred_element_type=F32)


def dot_t(a, b):
    return lax.dot_general(a, b, (((1,), (1,)), ((), ())), preferred_element_type=F32)


def t_dot(a, b):
    return lax.dot_general(a, b, (((0,), (0,)), ((), ())), preferred_element_type=F32)


SCALAR = pl.BlockSpec(memory_space=pltpu.SMEM)


def row_spec(block, width):
    return pl.BlockSpec((block, width), lambda i: (i, 0))


def full_spec(shape):
    return pl.BlockSpec(shape, lambda i: (0,) * len(shape))


def place(me, pieces, out_ref, sem_of):
    size = out_ref.shape[0] // CHUNKS
    h = size // 2
    for device in range(CHUNKS):
        mask = jnp.bitwise_xor(me, device)
        x, y, z = (mask >> 1) & 1, (mask >> 2) & 1, mask >> 3
        for side in range(2):
            k = ((x << 3 | y << 2) if side else (y << 3 | x << 2)) | z
            target = out_ref.at[pl.ds(device * size + side * h, h), :]
            for core in range(2):

                @pl.when(mask & 1 == core)
                def _():
                    piece = pieces[2 * core + side].at[k]
                    pltpu.make_async_copy(piece, target, sem_of(device)).start()


def project_kernel(me_ref, x_ref, *refs):
    pieces, (o_ref, w_ref, t_ref, sem) = refs[:4], refs[4:]
    j = pl.program_id(0)
    block = o_ref.shape[1]
    width = x_ref.shape[1]

    @pl.when(j == 0)
    def _():
        place(me_ref[0], pieces, w_ref, lambda device: sem)
        pltpu.make_async_copy(w_ref, w_ref, sem).wait()
        table = w_ref[:, 3 * width :].astype(F32).T
        t_ref[...] = table[: t_ref.shape[0]]

    per = width // block
    at = pl.multiple_of((j % per) * block, block)
    bias = jnp.where(
        j < per,
        t_ref[0:1, pl.ds(at, block)],
        jnp.where(j >= 2 * per, t_ref[1:2, pl.ds(at, block)], 0.0),
    )
    w = w_ref[:, pl.ds(pl.multiple_of(j * block, block), block)]
    o_ref[...] = (dot(x_ref[...], w) + bias).astype(BF16)


def project(me, x, pieces, block=1024):
    rows, width = x.shape
    cols = 3 * width
    held = pieces[0].shape[2]
    return pl.pallas_call(
        project_kernel,
        grid=(cols // block,),
        in_specs=[SCALAR, full_spec((rows, width))] + [pl.BlockSpec(memory_space=pl.ANY)] * 4,
        out_specs=[
            pl.BlockSpec((rows, block), lambda j: (0, j)),
            full_spec((width, held)),
            full_spec((16, width)),
        ],
        out_shape=[
            jax.ShapeDtypeStruct((rows, cols), BF16),
            jax.ShapeDtypeStruct((width, held), BF16),
            jax.ShapeDtypeStruct((16, width), F32),
        ],
        scratch_shapes=[pltpu.SemaphoreType.DMA],
        compiler_params=params(),
        cost_estimate=cost(2 * rows * width * cols, 2 * (rows * width + 2 * width * cols + rows * cols)),
        name="project",
    )(me, x, *pieces)


def head_mask(shape, h):
    lane = lax.broadcasted_iota(jnp.int32, shape, 1)
    return (lane >= h * HD) & (lane < (h + 1) * HD)


def attend_kernel(q_ref, k_ref, v_ref, *refs):
    ctx_ref, lse_ref = refs[-2:]
    q = q_ref[...] * jnp.asarray(1.0 / math.sqrt(HD), BF16)
    k = k_ref[...]
    vt = v_ref[...].T
    parts = []
    for h in range(2):
        qh = jnp.where(head_mask(q.shape, h), q, jnp.zeros_like(q))
        s = dot_t(k, qh)
        m = jnp.max(s, axis=0, keepdims=True)
        e = jnp.exp(s - m)
        total = jnp.sum(e, axis=0, keepdims=True)
        c = dot(vt[h * HD : (h + 1) * HD, :], e.astype(BF16))
        parts.append(c * (1.0 / total))
        lse_ref[0, 0, h : h + 1, :] = m + jnp.log(total)
    ctx_ref[...] = jnp.concatenate(parts, axis=0).T.astype(BF16)


def attend(qkv, width, start, n_pairs, held=()):
    rows = qkv.shape[0]
    count, pairs = rows // LEN, width // 128
    return pl.pallas_call(
        attend_kernel,
        grid=(n_pairs, count),
        in_specs=[
            pl.BlockSpec((LEN, 128), lambda p, s: (s, start + p)),
            pl.BlockSpec((LEN, 128), lambda p, s: (s, pairs + start + p)),
            pl.BlockSpec((LEN, 128), lambda p, s: (s, 2 * pairs + start + p)),
        ]
        + [pl.BlockSpec(memory_space=pl.ANY)] * len(held),
        out_specs=[
            pl.BlockSpec((LEN, 128), lambda p, s: (s, start + p)),
            pl.BlockSpec((1, 1, 2, LEN), lambda p, s: (start + p, s, 0, 0)),
        ],
        out_shape=[
            jax.ShapeDtypeStruct((rows, width), BF16),
            jax.ShapeDtypeStruct((pairs, count, 2, LEN), F32),
        ],
        input_output_aliases={3 + k: k for k in range(len(held))},
        compiler_params=params(),
        cost_estimate=cost(
            rows * n_pairs * LEN * 2048, 1024 * rows * n_pairs, rows * n_pairs * LEN * 2
        ),
        name="attend",
    )(qkv, qkv, qkv, *held)


def attend_back_kernel(q_ref, k_ref, v_ref, c_ref, d_ref, lse_ref, dp_ref, sq_ref, sv_ref):
    scale = 1.0 / math.sqrt(HD)
    q = q_ref[...] * jnp.asarray(scale, BF16)
    k = k_ref[...]
    v = v_ref[...]
    d = d_ref[...]
    kt = k.T
    prod = (d.astype(F32) * c_ref[...].astype(F32)).T
    dk = dv = None
    parts = []
    for h in range(2):
        mask = head_mask(q.shape, h)
        qh = jnp.where(mask, q, jnp.zeros_like(q))
        dh = jnp.where(mask, d, jnp.zeros_like(d))
        delta = jnp.sum(prod[h * HD : (h + 1) * HD, :], axis=0, keepdims=True)
        p = jnp.exp(dot_t(k, qh) - lse_ref[0, 0, h : h + 1, :])
        ds = (p * (dot_t(v, dh) - delta)).astype(BF16)
        dv_h = dot(p.astype(BF16), dh)
        dk_h = dot(ds, qh)
        dv = dv_h if dv is None else dv + dv_h
        dk = dk_h if dk is None else dk + dk_h
        parts.append(dot(kt[h * HD : (h + 1) * HD, :], ds) * scale)
    dq = jnp.concatenate(parts, axis=0).T.astype(BF16)
    dv = dv.astype(BF16)
    dp_ref[:, 0:128] = dq
    dp_ref[:, 128:256] = dk.astype(BF16)
    dp_ref[:, 256:384] = dv
    sq = jnp.sum(dq.astype(F32), axis=0, keepdims=True)
    sv = jnp.sum(dv.astype(F32), axis=0, keepdims=True)
    first = pl.program_id(1) == 0

    @pl.when(first)
    def _():
        sq_ref[...] = sq
        sv_ref[...] = sv

    @pl.when(jnp.logical_not(first))
    def _():
        sq_ref[...] += sq
        sv_ref[...] += sv


def attend_back(qkv, ctx, dctx, lse, width, start, n_pairs):
    rows = qkv.shape[0]
    count, pairs = rows // LEN, width // 128
    cols = n_pairs * 128
    sum_block = pl.BlockSpec((1, 128), lambda p, s: (0, p))
    return pl.pallas_call(
        attend_back_kernel,
        grid=(n_pairs, count),
        in_specs=[
            pl.BlockSpec((LEN, 128), lambda p, s: (s, start + p)),
            pl.BlockSpec((LEN, 128), lambda p, s: (s, pairs + start + p)),
            pl.BlockSpec((LEN, 128), lambda p, s: (s, 2 * pairs + start + p)),
            pl.BlockSpec((LEN, 128), lambda p, s: (s, start + p)),
            pl.BlockSpec((LEN, 128), lambda p, s: (s, start + p)),
            pl.BlockSpec((1, 1, 2, LEN), lambda p, s: (start + p, s, 0, 0)),
        ],
        out_specs=[pl.BlockSpec((LEN, 384), lambda p, s: (s, p)), sum_block, sum_block],
        out_shape=[jax.ShapeDtypeStruct((rows, 3 * cols), BF16)]
        + [jax.ShapeDtypeStruct((1, cols), F32)] * 2,
        compiler_params=params(),
        cost_estimate=cost(rows * cols * LEN * 10 * 4, 16 * rows * cols, rows * cols * LEN // HD),
        name="attend_back",
    )(qkv, qkv, qkv, ctx, dctx, lse)


def out_weight(held):
    _, rows, width = held.shape
    size = width // CHUNKS
    return pl.BlockSpec((CHUNKS, size, width), lambda i: (0, rows // size - 1, 0))


def up_weight(held):
    _, rows, width = held.shape
    return pl.BlockSpec((CHUNKS, rows - width // CHUNKS, width), lambda i: (0, 0, 0))


def out_norm_kernel(c_ref, w_ref, b_ref, x_ref, g_ref, s_ref, hat_ref, rstd_ref, low_ref):
    w = w_ref[...].reshape(-1, x_ref.shape[1])
    h = x_ref[...].astype(F32) + (dot(c_ref[...], w) + b_ref[...])
    center = h - jnp.mean(h, axis=-1, keepdims=True)
    rstd = lax.rsqrt(jnp.mean(center * center, axis=-1, keepdims=True) + EPS)
    hat = center * rstd
    hat_ref[...] = hat
    rstd_ref[...] = rstd
    low_ref[...] = (hat * g_ref[...] + s_ref[...]).astype(BF16)


def out_norm(ctx, held, bias, tokens, gain, shift, block=256):
    rows, width = tokens.shape
    vec = full_spec((1, width))
    return pl.pallas_call(
        out_norm_kernel,
        grid=(rows // block,),
        in_specs=[
            row_spec(block, width),
            out_weight(held),
            vec,
            row_spec(block, width),
            vec,
            vec,
        ],
        out_specs=[row_spec(block, width), row_spec(block, 1), row_spec(block, width)],
        out_shape=[
            jax.ShapeDtypeStruct((rows, width), F32),
            jax.ShapeDtypeStruct((rows, 1), F32),
            jax.ShapeDtypeStruct((rows, width), BF16),
        ],
        compiler_params=params(),
        cost_estimate=cost(2 * rows * width * width, 14 * rows * width),
        name="out_norm",
    )(ctx, held, bias, tokens, gain, shift)


ERF_P = 0.3275911 / math.sqrt(2.0)
ERF_A = (0.254829592, -0.284496736, 1.421413741, -1.453152027, 1.061405429)


def gelu_pair(u):
    t = 1.0 / (1.0 + ERF_P * jnp.abs(u))
    e = jnp.exp(-0.5 * (u * u))
    poly = t * (ERF_A[0] + t * (ERF_A[1] + t * (ERF_A[2] + t * (ERF_A[3] + t * ERF_A[4]))))
    tail = 0.5 * poly * e
    cdf = jnp.where(u >= 0, 1.0 - tail, tail)
    return u * cdf, cdf + u * e * (1.0 / math.sqrt(2.0 * math.pi))


def up_kernel(x_ref, w_ref, b_ref, *refs):
    act_ref, slope_ref = refs[-2:]
    block = act_ref.shape[1]
    u = dot(x_ref[...], w_ref[...].reshape(-1, block)) + b_ref[...]
    act, slope = gelu_pair(u)
    act_ref[...] = act.astype(BF16)
    slope_ref[...] = slope.astype(BF16)


def up_gelu(x, held, bias, half, done=(), block=512):
    rows, width = x.shape
    cols = bias.shape[1]
    per, steps = width // block, cols // block // 2
    first = half * steps
    col = pl.BlockSpec((rows, block), lambda j: (0, first + j))
    return pl.pallas_call(
        up_kernel,
        grid=(steps,),
        in_specs=[
            full_spec((rows, width)),
            pl.BlockSpec((CHUNKS, width // CHUNKS, block), lambda j: (0, (first + j) // per, (first + j) % per)),
            pl.BlockSpec((1, block), lambda j: (0, first + j)),
        ]
        + [pl.BlockSpec(memory_space=pl.ANY)] * len(done),
        out_specs=[col, col],
        out_shape=[jax.ShapeDtypeStruct((rows, cols), BF16)] * 2,
        input_output_aliases={3 + k: k for k in range(len(done))},
        compiler_params=params(),
        cost_estimate=cost(
            rows * width * cols, width * cols + 2 * rows * cols, rows * cols
        ),
        name="up_gelu",
    )(x, held, bias, *done)


def down_norm_kernel(
    me_ref, p0_ref, p1_ref, p2_ref, p3_ref,
    a_ref, b_ref, hat1_ref, g1_ref, s1_ref, g2_ref, s2_ref, cot_ref,
    out_ref, dh_ref, dm_ref, dg_ref, ds_ref, db_ref, w_ref, all_ref, acc_ref, sems, *, steps,
):
    j = pl.program_id(0)
    deep = all_ref.shape[0] // steps

    @pl.when(j == 0)
    def _():
        pieces = (p0_ref, p1_ref, p2_ref, p3_ref)
        place(me_ref[0], pieces, all_ref, lambda device: sems.at[device * steps // CHUNKS])
        dg_ref[...] = jnp.zeros_like(dg_ref)
        ds_ref[...] = jnp.zeros_like(ds_ref)
        db_ref[...] = jnp.zeros_like(db_ref)
        acc_ref[...] = jnp.zeros_like(acc_ref)

    @pl.when(j < steps)
    def _():
        part = all_ref.at[pl.ds(pl.multiple_of(j * deep, deep), deep), :]
        pltpu.make_async_copy(part, part, sems.at[j]).wait()
        w = part[...]
        w_ref[...] = w
        acc_ref[...] += dot(a_ref[...], w)

    @pl.when(j >= steps)
    def _():
        block = out_ref.shape[0]
        n1 = hat1_ref[...] * g1_ref[...] + s1_ref[...]
        mlp = acc_ref[pl.ds(pl.multiple_of((j - steps) * block, block), block), :]
        h = n1 + (mlp + b_ref[...])
        center = h - jnp.mean(h, axis=-1, keepdims=True)
        rstd = lax.rsqrt(jnp.mean(center * center, axis=-1, keepdims=True) + EPS)
        hat = center * rstd
        out_ref[...] = (hat * g2_ref[...] + s2_ref[...]).astype(BF16)
        cot = cot_ref[...].astype(F32)
        wide = cot * g2_ref[...]
        mean_a = jnp.mean(wide, axis=-1, keepdims=True)
        mean_b = jnp.mean(wide * hat, axis=-1, keepdims=True)
        dh = rstd * (wide - mean_a - hat * mean_b)
        dh_ref[...] = dh
        dm = dh.astype(BF16)
        dm_ref[...] = dm
        dg_ref[...] += jnp.sum(cot * hat, axis=0, keepdims=True)
        ds_ref[...] += jnp.sum(cot, axis=0, keepdims=True)
        db_ref[...] += jnp.sum(dm.astype(F32), axis=0, keepdims=True)


def down_norm(me, pieces, act, bias, hat1, g1, s1, g2, s2, cot, block=256, steps=4):
    rows, width = hat1.shape
    deep = act.shape[1]
    vec = full_spec((1, width))
    row = pl.BlockSpec((block, width), lambda j: (jnp.maximum(j - steps, 0), 0))
    return pl.pallas_call(
        functools.partial(down_norm_kernel, steps=steps),
        grid=(steps + rows // block,),
        in_specs=[SCALAR]
        + [pl.BlockSpec(memory_space=pl.ANY)] * 4
        + [pl.BlockSpec((rows, deep // steps), lambda j: (0, jnp.minimum(j, steps - 1)))]
        + [vec, row, vec, vec, vec, vec, row],
        out_specs=[row, row, row, vec, vec, vec]
        + [pl.BlockSpec((deep // steps, width), lambda j: (jnp.minimum(j, steps - 1), 0))],
        out_shape=[
            jax.ShapeDtypeStruct((rows, width), BF16),
            jax.ShapeDtypeStruct((rows, width), F32),
            jax.ShapeDtypeStruct((rows, width), BF16),
        ]
        + [jax.ShapeDtypeStruct((1, width), F32)] * 3
        + [jax.ShapeDtypeStruct((deep, width), BF16)],
        scratch_shapes=[
            pltpu.VMEM((deep, width), BF16),
            pltpu.VMEM((rows, width), F32),
            pltpu.SemaphoreType.DMA((steps,)),
        ],
        compiler_params=params(),
        cost_estimate=cost(2 * rows * width * deep, 2 * deep * (rows + width) + 14 * rows * width),
        name="down_norm",
    )(me, *pieces, act, bias, hat1, g1, s1, g2, s2, cot)


def split(value, core, chunk, keep_ref, send_ref):
    value = value.astype(BF16).reshape(-1, 2, 2, chunk // 2, value.shape[1])
    for half in range(2):
        even = value[:, 0, half].reshape(keep_ref.shape[1:])
        odd = value[:, 1, half].reshape(keep_ref.shape[1:])
        keep_ref[half] = jnp.where(core == 0, even, odd)
        send_ref[half] = jnp.where(core == 0, odd, even)


def join(keep, send, chunk):
    cols = keep.shape[-1]
    pair = [v.reshape(2, -1, chunk // 2, cols) for v in (keep, send)]
    return jnp.stack(pair, axis=0).transpose(2, 0, 1, 3, 4).reshape(-1, cols)


def down_grad_kernel(core_ref, a_ref, b_ref, keep_ref, send_ref):
    chunk = keep_ref.shape[1]
    split(t_dot(a_ref[...], b_ref[...]), core_ref[0], chunk, keep_ref, send_ref)


def down_grad(core, a, b):
    rows, deep = a.shape
    cols = b.shape[1]
    block = 4 * deep // CHUNKS
    out = pl.BlockSpec((2, block // 4, cols), lambda j: (0, j, 0))
    return pl.pallas_call(
        down_grad_kernel,
        grid=(deep // block,),
        in_specs=[SCALAR, pl.BlockSpec((rows, block), lambda j: (0, j)), full_spec((rows, cols))],
        out_specs=[out, out],
        out_shape=[jax.ShapeDtypeStruct((2, deep // 4, cols), BF16)] * 2,
        compiler_params=params(),
        cost_estimate=cost(2 * rows * deep * cols, 2 * (rows * deep + rows * cols + deep * cols)),
        name="down_grad",
    )(core, a, b)


def attn_grad_kernel(core_ref, xt_ref, *refs, n_parts, more):
    parts, rest = refs[:n_parts], refs[n_parts:]
    keep_ref, send_ref = rest[-2:]
    chunk = 32
    at = 0

    def put(value):
        nonlocal at
        cols = value.shape[1]
        here = [ref.at[:, :, at : at + cols] for ref in (keep_ref, send_ref)]
        split(value, core_ref[0], chunk, *here)
        at += cols

    for ref in parts:
        put(dot(xt_ref[...], ref[...]))
    if more == "out":
        put(t_dot(rest[0][...], rest[1][...]))
    else:
        put(rest[0][...])


def attn_grad(core, xt, parts, extra, more, block=256):
    width, rows = xt.shape
    in_specs = [SCALAR, row_spec(block, rows)] + [full_spec(p.shape) for p in parts]
    cols = sum(p.shape[1] for p in parts)
    if more == "out":
        in_specs += [pl.BlockSpec((rows, block), lambda i: (0, i)), full_spec(extra[1].shape)]
        cols += extra[1].shape[1]
    else:
        in_specs += [row_spec(block, extra[0].shape[1])]
        cols += extra[0].shape[1]
    out = pl.BlockSpec((2, block // 4, cols), lambda i: (0, i, 0))
    return pl.pallas_call(
        functools.partial(attn_grad_kernel, n_parts=len(parts), more=more),
        grid=(width // block,),
        in_specs=in_specs,
        out_specs=[out, out],
        out_shape=[jax.ShapeDtypeStruct((2, width // 4, cols), BF16)] * 2,
        compiler_params=params(),
        cost_estimate=cost(2 * rows * width * cols, 2 * (rows * width + cols * (rows + width))),
        name="attn_grad",
    )(core, xt, *parts, *extra)


def up_back_kernel(
    core_ref, dm_ref, w_ref, slope_ref, x_ref, du_ref, keep_ref, send_ref, db_ref, xt_ref
):
    @pl.when(pl.program_id(0) == 0)
    def _():
        xt_ref[...] = x_ref[...].T

    du = (dot_t(dm_ref[...], w_ref[...]) * slope_ref[...].astype(F32)).astype(BF16)
    du_ref[...] = du
    db_ref[...] = jnp.sum(du.astype(F32), axis=0, keepdims=True)
    split(dot(xt_ref[...], du), core_ref[0], xt_ref.shape[0] // CHUNKS, keep_ref, send_ref)


def up_back(core, dm, w_down, slope, x):
    rows, width = dm.shape
    deep = slope.shape[1]
    block = 4 * deep // CHUNKS
    col = pl.BlockSpec((rows, block), lambda j: (0, j))
    half = pl.BlockSpec((2, width // 4, block), lambda j: (0, 0, j))
    return pl.pallas_call(
        up_back_kernel,
        grid=(deep // block,),
        in_specs=[
            SCALAR,
            full_spec((rows, width)),
            pl.BlockSpec((block, width), lambda j: (j, 0)),
            col,
            full_spec((rows, width)),
        ],
        out_specs=[col, half, half, pl.BlockSpec((1, block), lambda j: (0, j))],
        out_shape=[
            jax.ShapeDtypeStruct((rows, deep), BF16),
            jax.ShapeDtypeStruct((2, width // 4, deep), BF16),
            jax.ShapeDtypeStruct((2, width // 4, deep), BF16),
            jax.ShapeDtypeStruct((1, deep), F32),
        ],
        scratch_shapes=[pltpu.VMEM((width, rows), BF16)],
        compiler_params=params(),
        cost_estimate=cost(4 * rows * width * deep, 4 * deep * (rows + width) + 4 * rows * width),
        name="up_back",
    )(core, dm, w_down, slope, x)


def norm_back_kernel(
    du_ref, w_ref, out_ref, dh2_ref, hat_ref, rstd_ref, g_ref,
    dh_ref, da_ref, dc_ref, dg_ref, ds_ref, db_ref,
):
    width = dh2_ref.shape[1]
    dn = dh2_ref[...]
    size = width // CHUNKS
    for j in range(du_ref.shape[1] // width):
        w = w_ref[:, j * size : (j + 1) * size, :].reshape(width, width)
        dn = dn + dot_t(du_ref[:, j * width : (j + 1) * width], w)
    hat = hat_ref[...]
    wide = dn * g_ref[...]
    mean_a = jnp.mean(wide, axis=-1, keepdims=True)
    mean_b = jnp.mean(wide * hat, axis=-1, keepdims=True)
    dh = rstd_ref[...] * (wide - mean_a - hat * mean_b)
    dh_ref[...] = dh
    da = dh.astype(BF16)
    da_ref[...] = da
    dc_ref[...] = dot_t(da, out_ref[...].reshape(width, width)).astype(BF16)

    @pl.when(pl.program_id(0) == 0)
    def _():
        dg_ref[...] = jnp.zeros_like(dg_ref)
        ds_ref[...] = jnp.zeros_like(ds_ref)
        db_ref[...] = jnp.zeros_like(db_ref)

    dg_ref[...] += jnp.sum(dn * hat, axis=0, keepdims=True)
    ds_ref[...] += jnp.sum(dn, axis=0, keepdims=True)
    db_ref[...] += jnp.sum(da.astype(F32), axis=0, keepdims=True)


def norm_back(du, held, dh2, hat, rstd, gain, block=256):
    rows, width = hat.shape
    deep = du.shape[1]
    vec = full_spec((1, width))
    row = row_spec(block, width)
    return pl.pallas_call(
        norm_back_kernel,
        grid=(rows // block,),
        in_specs=[row_spec(block, deep), up_weight(held), out_weight(held)]
        + [row, row, row_spec(block, 1), vec],
        out_specs=[row, row, row, vec, vec, vec],
        out_shape=[
            jax.ShapeDtypeStruct((rows, width), F32),
            jax.ShapeDtypeStruct((rows, width), BF16),
            jax.ShapeDtypeStruct((rows, width), BF16),
        ]
        + [jax.ShapeDtypeStruct((1, width), F32)] * 3,
        compiler_params=params(),
        cost_estimate=cost(2 * rows * width * deep, 2 * deep * (rows + width) + 14 * rows * width),
        name="norm_back",
    )(du, held, held, dh2, hat, rstd, gain)


def input_back_kernel(*refs):
    *parts, w_ref, dh_ref, o_ref = refs
    width = o_ref.shape[1]
    total = dh_ref[...]
    for which in range(3):
        pieces = [
            ref[:, at : at + 128]
            for ref in parts
            for at in range(which * 128, ref.shape[1], 384)
        ]
        col = which * width
        total = total + dot_t(jnp.concatenate(pieces, axis=1), w_ref[:, col : col + width])
    o_ref[...] = total.astype(BF16)


def input_back(parts, w, dh, block=256):
    rows, width = dh.shape
    return pl.pallas_call(
        input_back_kernel,
        grid=(rows // block,),
        in_specs=[row_spec(block, p.shape[1]) for p in parts]
        + [pl.BlockSpec((width, 3 * width), lambda i: (0, 0)), row_spec(block, width)],
        out_specs=row_spec(block, width),
        out_shape=jax.ShapeDtypeStruct((rows, width), BF16),
        compiler_params=params(),
        cost_estimate=cost(6 * rows * width * width, 18 * rows * width),
        name="input_back",
    )(*parts, w, dh)


def exchange(x, n, mask):
    return lax.ppermute(x, "dp", [(i, i ^ mask) for i in range(n)])


def pick(x, axis, index):
    return lax.dynamic_index_in_dim(x, index, axis, keepdims=False)


def tie(*values):
    return lax.optimization_barrier(values)


class Scatter:
    def __init__(self, keep, send, n, r):
        self.n, self.h, self.me, self.cols = n, r // 2, lax.axis_index("dp"), keep.shape[-1]
        self.keep, self.got = keep, exchange(send, n, 1)
        self.left = [[4, 3, 2, 1], [4, 3, 2, 1]]
        self.step = 0

    def part(self, side, bit, which):
        left = self.left[side]
        at, size = left.index(bit), 1 << len(left)
        shape = (1 << at, 2, size >> (at + 1), self.h, self.cols)
        total = None
        for value in self.held[side]:
            lead = value.size // math.prod(shape)
            value = value.reshape(lead, *shape)
            start = (side if lead == 2 else 0, 0, which, 0, 0, 0)
            value = lax.dynamic_slice(value, start, (1, shape[0], 1, *shape[2:])).astype(F32)
            total = value if total is None else total + value
        return total.reshape(size // 2, self.h, self.cols)

    def behind(self, along):
        if self.step == 0:
            flat = tie(self.keep, self.got, *along)
            self.held = [flat[:2]] * 2
            return flat[2:]
        flat = tie(*self.held[0], *self.held[1], *along)
        self.held = [flat[:2], flat[2:4]]
        return flat[4:]

    def halve(self, *along):
        along = self.behind(along)
        bits = ((2, 1), (1, 2))
        sums = []
        for side in range(2):
            bit = bits[side][self.step]
            mine = (self.me >> bit) & 1
            sums += [self.part(side, bit, which).astype(BF16) for which in (1 - mine, mine)]
        *sums, = tie(*sums, *along)
        sums, along = sums[:4], sums[4:]
        for side in range(2):
            bit = bits[side][self.step]
            self.held[side] = (sums[2 * side + 1], exchange(sums[2 * side], self.n, 1 << bit))
            self.left[side].remove(bit)
        self.step += 1
        return along[0] if len(along) == 1 else along

    def column_one(self, *along):
        along = self.behind(along)
        mine = self.me >> 4
        sent, kept = [
            jnp.concatenate([self.part(side, 4, which) for side in range(2)], axis=1).astype(BF16)
            for which in (1 - mine, mine)
        ]
        sent, kept, *along = tie(sent, kept, *along)
        self.pair = (kept, exchange(sent, self.n, 16))
        return along[0] if len(along) == 1 else along

    def column_two(self, *along):
        *self.pair, = tie(*self.pair, *along)
        self.pair, along = self.pair[:2], self.pair[2:]
        mine = (self.me >> 3) & 1
        sent, kept = [
            sum(pick(value, 0, which).astype(F32) for value in self.pair) for which in (1 - mine, mine)
        ]
        sent, kept, *along = tie(sent.astype(BF16), kept, *along)
        self.last = [kept, exchange(sent, self.n, 8)]
        return along[0] if len(along) == 1 else along

    def column(self, *along):
        along = self.behind(along)
        mine = self.me >> 3
        sums = [
            jnp.concatenate(
                [
                    sum(pick(v, 0, mine ^ k).astype(F32) for v in self.held[side])
                    for side in range(2)
                ],
                axis=0,
            )
            for k in range(4)
        ]
        *sums, = tie(sums[0], *[v.astype(BF16) for v in sums[1:]], *along)
        sums, along = sums[:4], sums[4:]
        self.last = sums[:1] + [exchange(sums[k], self.n, k << 3) for k in (1, 2, 3)]
        return along[0] if len(along) == 1 else along

    def after(self, *along):
        flat = tie(*self.last, *along)
        self.last, along = flat[: len(self.last)], flat[len(self.last) :]
        return along[0] if len(along) == 1 else along

    def result(self):
        return sum(value.astype(F32) for value in self.last)


class PlainScatter:
    def __init__(self, keep, send, n, r):
        self.keep = keep
        whole = join(keep, send, keep.shape[1] * 4 // CHUNKS)
        self.total = lax.psum_scatter(whole.astype(F32), "dp", scatter_dimension=0, tiled=True)

    def halve(self, *along):
        return along[0] if len(along) == 1 else along

    column = column_one = column_two = after = halve

    def result(self):
        return self.total


def gather(x):
    return lax.all_gather(x, "dp", axis=0, tiled=True)


class Gather:
    def __init__(self, x, n):
        self.n, self.shape = n, x.shape
        self.near = [x] + [exchange(x, n, k << 3) for k in (1, 2, 3)]

    def after(self, *along):
        flat = tie(*self.near, *along)
        self.near = flat[: len(self.near)]
        along = flat[len(self.near) :]
        return along[0] if len(along) == 1 else along

    def column(self, *along):
        h = self.shape[0] // 2
        sides = [jnp.concatenate([v[at : at + h] for v in self.near], axis=0) for at in (0, h)]
        *sides, = tie(*sides, *along)
        self.near = [sides[0], exchange(sides[0], self.n, 2), sides[1], exchange(sides[1], self.n, 4)]
        along = sides[2:]
        return along[0] if len(along) == 1 else along

    def join(self):
        return [jnp.concatenate(self.near[k : k + 2], axis=0) for k in (0, 2)]

    def plane(self, *along):
        sides = self.join()
        *sides, = tie(*sides, *along)
        self.near = [sides[0], exchange(sides[0], self.n, 4), sides[1], exchange(sides[1], self.n, 2)]
        along = sides[2:]
        return along[0] if len(along) == 1 else along

    def pair(self, *along):
        sides = self.join()
        *sides, = tie(*sides, *along)
        pieces = sides[:2] + [exchange(v, self.n, 1) for v in sides[:2]]
        pieces = [v.reshape(16, self.shape[0] // 2, self.shape[1]) for v in pieces]
        return pieces, *sides[2:]


def plain_pieces(whole, size):
    chips = whole.reshape(4, 2, 2, 2, 2, size // 2, whole.shape[1])
    upper = chips[:, :, :, :, 0].transpose(3, 1, 2, 0, 4, 5)
    lower = chips[:, :, :, :, 1].transpose(3, 2, 1, 0, 4, 5)
    return [v[core].reshape(16, size // 2, -1) for core in range(2) for v in (upper, lower)]


def columns(vector, r):
    return vector.reshape(-1, r).T


def table_of(vectors, n, r):
    parts = [v.reshape(n, -1, r).transpose(0, 2, 1).reshape(n * r, -1) for v in vectors]
    return jnp.concatenate(parts, axis=1)


def local(
    n,
    tokens,
    cotangent,
    w_qkv,
    q_bias,
    v_bias,
    w_out,
    out_bias,
    attn_gain,
    attn_shift,
    w_up,
    up_bias,
    w_down,
    down_bias,
    mlp_gain,
    mlp_shift,
):
    rows, width = tokens.shape
    r = w_qkv.shape[0]
    wide = w_up.shape[1] // width
    vectors = (
        q_bias, v_bias, out_bias, attn_gain, attn_shift, down_bias, mlp_gain, mlp_shift, up_bias,
    )
    small = jnp.concatenate([columns(v, r) for v in vectors], axis=1)
    small = jnp.pad(small, ((0, 0), (0, 128 - small.shape[1])))
    first = jnp.concatenate([w_qkv, small], axis=1)
    tokens_t = tokens.T
    core, me, pairs = jnp.int32(0), jnp.int32(0), width // 128
    if n == CHUNKS:
        scatter, me = Scatter, lax.axis_index("dp")
        core = me & 1
        blocks = [w_up[:, j * width : (j + 1) * width] for j in range(wide)]
        held = gather(jnp.concatenate(blocks + [w_out], axis=0)).reshape(CHUNKS, -1, width)
        first = Gather(first, n)
        first.column()
        first.plane()
        pieces, tokens_t, w_down_share = first.pair(tokens_t, w_down)
        second = Gather(w_down_share, n)
    else:
        scatter = PlainScatter
        up = gather(w_up).reshape(CHUNKS, width // CHUNKS, wide, width).transpose(0, 2, 1, 3)
        up = up.reshape(CHUNKS, wide * width // CHUNKS, width)
        out = gather(w_out).reshape(CHUNKS, width // CHUNKS, width)
        held = jnp.concatenate([up, out], axis=1)
        pieces = plain_pieces(gather(first), width // CHUNKS)
        down_pieces = plain_pieces(gather(w_down), wide * width // CHUNKS)
    core, me = core.reshape(1), me.reshape(1)

    qkv, w_full, table = project(me, tokens, pieces)
    ob, g1, s1, db, g2, s2 = [table[j : j + 1] for j in range(2, 8)]
    ub = table[8 : 8 + wide].reshape(wide, CHUNKS, -1).transpose(1, 0, 2).reshape(1, -1)
    half = pairs // 2
    ctx, lse = attend(qkv, width, 0, half)
    if n == CHUNKS:
        ctx = second.column(second.after(ctx))
    ctx, lse = attend(qkv, width, half, pairs - half, (ctx, lse))
    if n == CHUNKS:
        ctx = second.plane(second.after(ctx))
    hat1, rstd1, n1_low = out_norm(ctx, held, ob, tokens, g1, s1)
    act, slope = up_gelu(n1_low, held, ub, 0)
    if n == CHUNKS:
        down_pieces, act = second.pair(second.after(act))
    act, slope = up_gelu(n1_low, held, ub, 1, (act, slope))
    layer_out, dh2, dm, d_g2, d_s2, d_db, full_down = down_norm(
        me, down_pieces, act, db, hat1, g1, s1, g2, s2, cotangent
    )

    sums = {}

    def at(name, *along):
        for who, step in PLAN[name]:
            along = getattr(sums[who], step)(*along)
            along = along if type(along) in (tuple, list) else (along,)
        return along

    def back(k):
        return attend_back(qkv, ctx, dctx, lse, width, sum(PARTS[:k]), PARTS[k])

    sums["D"] = scatter(*down_grad(core, act, dm), n, w_down.shape[0])
    du, keep, send, d_ub = up_back(core, dm, full_down, slope, n1_low)
    sums["U"] = scatter(keep, send, n, r)
    (du,) = at("up_back", du)
    dh1, da, dctx, d_g1, d_s1, d_ob = norm_back(du, held, dh2, hat1, rstd1, g1)
    (dctx,) = at("norm_back", dctx)
    first, sq0, sv0 = back(0)
    (first,) = at("first", first)
    keep, send = attn_grad(core, tokens_t, [first], [ctx, da], "out")
    sums["E"] = scatter(keep, send, n, r)
    keep, dctx = at("early", sums["E"].keep, dctx)
    sums["E"].keep = keep
    second, sq1, sv1 = back(1)
    second, dctx = at("second", second, dctx)
    third, sq2, sv2 = back(2)
    (third,) = at("third", third)
    d_qb = jnp.concatenate([sq0, sq1, sq2], axis=1)
    d_vb = jnp.concatenate([sv0, sv1, sv2], axis=1)
    d_small = table_of([d_qb, d_vb, d_ob, d_g1, d_s1, d_db, d_g2, d_s2, d_ub], CHUNKS, width // CHUNKS)
    d_small = jnp.pad(d_small, ((0, 0), (0, 128 - d_small.shape[1]))).astype(BF16)
    keep, send = attn_grad(core, tokens_t, [second, third], [d_small], "small")
    sums["L"] = scatter(keep, send, n, r)
    keep, dh1 = at("late", sums["L"].keep, dh1)
    sums["L"].keep = keep
    input_grad = input_back([first, second, third], w_full, dh1)
    (input_grad,) = at("input_back", input_grad)
    down_sum, up_sum, early_sum, late_sum = [sums[k] for k in "DUEL"]

    early, late = early_sum.result(), late_sum.result()
    qkv_cols = PARTS[0] * 384
    d_qkv = jnp.concatenate([early[:, :qkv_cols], late[:, : 3 * width - qkv_cols]], axis=1)
    d_qkv = d_qkv.reshape(r, pairs, 3, 128).transpose(0, 2, 1, 3).reshape(r, 3 * width)
    d_out = early[:, qkv_cols:]
    d_small = late[:, 3 * width - qkv_cols :]

    def vector(start, k=1):
        return d_small[:, start : start + k].T.reshape(-1)

    d_qb, d_vb, d_ob, d_g1, d_s1, d_db, d_g2, d_s2 = [vector(j) for j in range(8)]
    d_ub = d_small[:, 8 : 8 + wide]
    d_ub = d_ub.T.reshape(-1)
    return (
        layer_out, input_grad, d_qkv, d_qb, d_vb, d_out, d_ob, d_g1, d_s1,
        up_sum.result(), d_ub, down_sum.result(), d_db, d_g2, d_s2,
    )


def solution(mesh):
    flat, square = P("dp"), P("dp", None)
    in_specs = (
        square, square, square, flat, flat, square, flat, flat, flat,
        square, flat, square, flat, flat, flat,
    )
    return jax.shard_map(
        functools.partial(local, mesh.shape["dp"]),
        mesh=mesh,
        in_specs=in_specs,
        out_specs=in_specs,
        check_vma=False,
    )
```

```python
import functools
import math

import jax
import jax.numpy as jnp
from jax import lax
from jax.experimental import pallas as pl
from jax.experimental.pallas import tpu as pltpu
from jax.sharding import PartitionSpec as P

HD = 64
LEN = 512
EPS = 1e-05
CHUNKS = 32
F32 = jnp.float32
BF16 = jnp.bfloat16
MIB = 1 << 20


def params(limit=48):
    return pltpu.CompilerParams(vmem_limit_bytes=limit * MIB)


COST = 0.02
PARTS = (3, 3, 2)
PLAN = {
    "up_back": [("D", "halve")],
    "norm_back": [("D", "halve"), ("U", "halve")],
    "first": [],
    "early": [("D", "column"), ("U", "halve")],
    "second": [("E", "halve")],
    "third": [("D", "after"), ("U", "column"), ("E", "halve")],
    "late": [("L", "halve")],
    "input_back": [("L", "halve"), ("U", "after"), ("E", "column"), ("L", "column")],
}


def cost(flops, nbytes, trans=0):
    return pl.CostEstimate(
        flops=int(COST * flops), bytes_accessed=int(COST * nbytes), transcendentals=int(COST * trans)
    )


def dot(a, b):
    return jnp.dot(a, b, preferred_element_type=F32)


def dot_t(a, b):
    return lax.dot_general(a, b, (((1,), (1,)), ((), ())), preferred_element_type=F32)


def t_dot(a, b):
    return lax.dot_general(a, b, (((0,), (0,)), ((), ())), preferred_element_type=F32)


SCALAR = pl.BlockSpec(memory_space=pltpu.SMEM)


def row_spec(block, width):
    return pl.BlockSpec((block, width), lambda i: (i, 0))


def full_spec(shape):
    return pl.BlockSpec(shape, lambda i: (0,) * len(shape))


def place(me, pieces, out_ref, sem_of):
    size = out_ref.shape[0] // CHUNKS
    h = size // 2
    for device in range(CHUNKS):
        mask = jnp.bitwise_xor(me, device)
        x, y, z = (mask >> 1) & 1, (mask >> 2) & 1, mask >> 3
        for side in range(2):
            k = ((x << 3 | y << 2) if side else (y << 3 | x << 2)) | z
            target = out_ref.at[pl.ds(device * size + side * h, h), :]
            for core in range(2):

                @pl.when(mask & 1 == core)
                def _():
                    piece = pieces[2 * core + side].at[k]
                    pltpu.make_async_copy(piece, target, sem_of(device)).start()


def project_kernel(me_ref, x_ref, *refs):
    pieces, (o_ref, w_ref, t_ref, sem) = refs[:4], refs[4:]
    j = pl.program_id(0)
    block = o_ref.shape[1]
    width = x_ref.shape[1]

    @pl.when(j == 0)
    def _():
        place(me_ref[0], pieces, w_ref, lambda device: sem)
        pltpu.make_async_copy(w_ref, w_ref, sem).wait()
        table = w_ref[:, 3 * width :].astype(F32).T
        t_ref[...] = table[: t_ref.shape[0]]

    per = width // block
    at = pl.multiple_of((j % per) * block, block)
    bias = jnp.where(
        j < per,
        t_ref[0:1, pl.ds(at, block)],
        jnp.where(j >= 2 * per, t_ref[1:2, pl.ds(at, block)], 0.0),
    )
    w = w_ref[:, pl.ds(pl.multiple_of(j * block, block), block)]
    o_ref[...] = (dot(x_ref[...], w) + bias).astype(BF16)


def project(me, x, pieces, block=1024):
    rows, width = x.shape
    cols = 3 * width
    held = pieces[0].shape[2]
    return pl.pallas_call(
        project_kernel,
        grid=(cols // block,),
        in_specs=[SCALAR, full_spec((rows, width))] + [pl.BlockSpec(memory_space=pl.ANY)] * 4,
        out_specs=[
            pl.BlockSpec((rows, block), lambda j: (0, j)),
            full_spec((width, held)),
            full_spec((16, width)),
        ],
        out_shape=[
            jax.ShapeDtypeStruct((rows, cols), BF16),
            jax.ShapeDtypeStruct((width, held), BF16),
            jax.ShapeDtypeStruct((16, width), F32),
        ],
        scratch_shapes=[pltpu.SemaphoreType.DMA],
        compiler_params=params(),
        cost_estimate=cost(2 * rows * width * cols, 2 * (rows * width + 2 * width * cols + rows * cols)),
        name="project",
    )(me, x, *pieces)


def head_mask(shape, h):
    lane = lax.broadcasted_iota(jnp.int32, shape, 1)
    return (lane >= h * HD) & (lane < (h + 1) * HD)


def attend_kernel(q_ref, k_ref, v_ref, *refs):
    ctx_ref, lse_ref = refs[-2:]
    q = q_ref[...] * jnp.asarray(1.0 / math.sqrt(HD), BF16)
    k = k_ref[...]
    vt = v_ref[...].T
    parts = []
    for h in range(2):
        qh = jnp.where(head_mask(q.shape, h), q, jnp.zeros_like(q))
        s = dot_t(k, qh)
        m = jnp.max(s, axis=0, keepdims=True)
        e = jnp.exp(s - m)
        total = jnp.sum(e, axis=0, keepdims=True)
        c = dot(vt[h * HD : (h + 1) * HD, :], e.astype(BF16))
        parts.append(c * (1.0 / total))
        lse_ref[0, 0, h : h + 1, :] = m + jnp.log(total)
    ctx_ref[...] = jnp.concatenate(parts, axis=0).T.astype(BF16)


def attend(qkv, width, start, n_pairs, held=()):
    rows = qkv.shape[0]
    count, pairs = rows // LEN, width // 128
    return pl.pallas_call(
        attend_kernel,
        grid=(n_pairs, count),
        in_specs=[
            pl.BlockSpec((LEN, 128), lambda p, s: (s, start + p)),
            pl.BlockSpec((LEN, 128), lambda p, s: (s, pairs + start + p)),
            pl.BlockSpec((LEN, 128), lambda p, s: (s, 2 * pairs + start + p)),
        ]
        + [pl.BlockSpec(memory_space=pl.ANY)] * len(held),
        out_specs=[
            pl.BlockSpec((LEN, 128), lambda p, s: (s, start + p)),
            pl.BlockSpec((1, 1, 2, LEN), lambda p, s: (start + p, s, 0, 0)),
        ],
        out_shape=[
            jax.ShapeDtypeStruct((rows, width), BF16),
            jax.ShapeDtypeStruct((pairs, count, 2, LEN), F32),
        ],
        input_output_aliases={3 + k: k for k in range(len(held))},
        compiler_params=params(),
        cost_estimate=cost(
            rows * n_pairs * LEN * 2048, 1024 * rows * n_pairs, rows * n_pairs * LEN * 2
        ),
        name="attend",
    )(qkv, qkv, qkv, *held)


def attend_back_kernel(q_ref, k_ref, v_ref, c_ref, d_ref, lse_ref, dp_ref, sq_ref, sv_ref):
    scale = 1.0 / math.sqrt(HD)
    q = q_ref[...] * jnp.asarray(scale, BF16)
    k = k_ref[...]
    v = v_ref[...]
    d = d_ref[...]
    kt = k.T
    prod = (d.astype(F32) * c_ref[...].astype(F32)).T
    dk = dv = None
    parts = []
    for h in range(2):
        mask = head_mask(q.shape, h)
        qh = jnp.where(mask, q, jnp.zeros_like(q))
        dh = jnp.where(mask, d, jnp.zeros_like(d))
        delta = jnp.sum(prod[h * HD : (h + 1) * HD, :], axis=0, keepdims=True)
        p = jnp.exp(dot_t(k, qh) - lse_ref[0, 0, h : h + 1, :])
        ds = (p * (dot_t(v, dh) - delta)).astype(BF16)
        dv_h = dot(p.astype(BF16), dh)
        dk_h = dot(ds, qh)
        dv = dv_h if dv is None else dv + dv_h
        dk = dk_h if dk is None else dk + dk_h
        parts.append(dot(kt[h * HD : (h + 1) * HD, :], ds) * scale)
    dq = jnp.concatenate(parts, axis=0).T.astype(BF16)
    dv = dv.astype(BF16)
    dp_ref[:, 0:128] = dq
    dp_ref[:, 128:256] = dk.astype(BF16)
    dp_ref[:, 256:384] = dv
    sq = jnp.sum(dq.astype(F32), axis=0, keepdims=True)
    sv = jnp.sum(dv.astype(F32), axis=0, keepdims=True)
    first = pl.program_id(1) == 0

    @pl.when(first)
    def _():
        sq_ref[...] = sq
        sv_ref[...] = sv

    @pl.when(jnp.logical_not(first))
    def _():
        sq_ref[...] += sq
        sv_ref[...] += sv


def attend_back(qkv, ctx, dctx, lse, width, start, n_pairs):
    rows = qkv.shape[0]
    count, pairs = rows // LEN, width // 128
    cols = n_pairs * 128
    sum_block = pl.BlockSpec((1, 128), lambda p, s: (0, p))
    return pl.pallas_call(
        attend_back_kernel,
        grid=(n_pairs, count),
        in_specs=[
            pl.BlockSpec((LEN, 128), lambda p, s: (s, start + p)),
            pl.BlockSpec((LEN, 128), lambda p, s: (s, pairs + start + p)),
            pl.BlockSpec((LEN, 128), lambda p, s: (s, 2 * pairs + start + p)),
            pl.BlockSpec((LEN, 128), lambda p, s: (s, start + p)),
            pl.BlockSpec((LEN, 128), lambda p, s: (s, start + p)),
            pl.BlockSpec((1, 1, 2, LEN), lambda p, s: (start + p, s, 0, 0)),
        ],
        out_specs=[pl.BlockSpec((LEN, 384), lambda p, s: (s, p)), sum_block, sum_block],
        out_shape=[jax.ShapeDtypeStruct((rows, 3 * cols), BF16)]
        + [jax.ShapeDtypeStruct((1, cols), F32)] * 2,
        compiler_params=params(),
        cost_estimate=cost(rows * cols * LEN * 10 * 4, 16 * rows * cols, rows * cols * LEN // HD),
        name="attend_back",
    )(qkv, qkv, qkv, ctx, dctx, lse)


def out_weight(held):
    _, rows, width = held.shape
    size = width // CHUNKS
    return pl.BlockSpec((CHUNKS, size, width), lambda i: (0, rows // size - 1, 0))


def up_weight(held):
    _, rows, width = held.shape
    return pl.BlockSpec((CHUNKS, rows - width // CHUNKS, width), lambda i: (0, 0, 0))


def out_norm_kernel(c_ref, w_ref, b_ref, x_ref, g_ref, s_ref, hat_ref, rstd_ref, low_ref):
    w = w_ref[...].reshape(-1, x_ref.shape[1])
    h = x_ref[...].astype(F32) + (dot(c_ref[...], w) + b_ref[...])
    center = h - jnp.mean(h, axis=-1, keepdims=True)
    rstd = lax.rsqrt(jnp.mean(center * center, axis=-1, keepdims=True) + EPS)
    hat = center * rstd
    hat_ref[...] = hat
    rstd_ref[...] = rstd
    low_ref[...] = (hat * g_ref[...] + s_ref[...]).astype(BF16)


def out_norm(ctx, held, bias, tokens, gain, shift, block=256):
    rows, width = tokens.shape
    vec = full_spec((1, width))
    return pl.pallas_call(
        out_norm_kernel,
        grid=(rows // block,),
        in_specs=[
            row_spec(block, width),
            out_weight(held),
            vec,
            row_spec(block, width),
            vec,
            vec,
        ],
        out_specs=[row_spec(block, width), row_spec(block, 1), row_spec(block, width)],
        out_shape=[
            jax.ShapeDtypeStruct((rows, width), F32),
            jax.ShapeDtypeStruct((rows, 1), F32),
            jax.ShapeDtypeStruct((rows, width), BF16),
        ],
        compiler_params=params(),
        cost_estimate=cost(2 * rows * width * width, 14 * rows * width),
        name="out_norm",
    )(ctx, held, bias, tokens, gain, shift)


ERF_P = 0.3275911 / math.sqrt(2.0)
ERF_A = (0.254829592, -0.284496736, 1.421413741, -1.453152027, 1.061405429)


def gelu_pair(u):
    t = 1.0 / (1.0 + ERF_P * jnp.abs(u))
    e = jnp.exp(-0.5 * (u * u))
    poly = t * (ERF_A[0] + t * (ERF_A[1] + t * (ERF_A[2] + t * (ERF_A[3] + t * ERF_A[4]))))
    tail = 0.5 * poly * e
    cdf = jnp.where(u >= 0, 1.0 - tail, tail)
    return u * cdf, cdf + u * e * (1.0 / math.sqrt(2.0 * math.pi))


def up_kernel(x_ref, w_ref, b_ref, *refs):
    act_ref, slope_ref = refs[-2:]
    block = act_ref.shape[1]
    u = dot(x_ref[...], w_ref[...].reshape(-1, block)) + b_ref[...]
    act, slope = gelu_pair(u)
    act_ref[...] = act.astype(BF16)
    slope_ref[...] = slope.astype(BF16)


def up_gelu(x, held, bias, half, done=(), block=512):
    rows, width = x.shape
    cols = bias.shape[1]
    per, steps = width // block, cols // block // 2
    first = half * steps
    col = pl.BlockSpec((rows, block), lambda j: (0, first + j))
    return pl.pallas_call(
        up_kernel,
        grid=(steps,),
        in_specs=[
            full_spec((rows, width)),
            pl.BlockSpec((CHUNKS, width // CHUNKS, block), lambda j: (0, (first + j) // per, (first + j) % per)),
            pl.BlockSpec((1, block), lambda j: (0, first + j)),
        ]
        + [pl.BlockSpec(memory_space=pl.ANY)] * len(done),
        out_specs=[col, col],
        out_shape=[jax.ShapeDtypeStruct((rows, cols), BF16)] * 2,
        input_output_aliases={3 + k: k for k in range(len(done))},
        compiler_params=params(),
        cost_estimate=cost(
            rows * width * cols, width * cols + 2 * rows * cols, rows * cols
        ),
        name="up_gelu",
    )(x, held, bias, *done)


def down_norm_kernel(
    me_ref, p0_ref, p1_ref, p2_ref, p3_ref,
    a_ref, b_ref, hat1_ref, g1_ref, s1_ref, g2_ref, s2_ref, cot_ref,
    out_ref, dh_ref, dm_ref, dg_ref, ds_ref, db_ref, w_ref, all_ref, acc_ref, sems, *, steps,
):
    j = pl.program_id(0)
    deep = all_ref.shape[0] // steps

    @pl.when(j == 0)
    def _():
        pieces = (p0_ref, p1_ref, p2_ref, p3_ref)
        place(me_ref[0], pieces, all_ref, lambda device: sems.at[device * steps // CHUNKS])
        dg_ref[...] = jnp.zeros_like(dg_ref)
        ds_ref[...] = jnp.zeros_like(ds_ref)
        db_ref[...] = jnp.zeros_like(db_ref)
        acc_ref[...] = jnp.zeros_like(acc_ref)

    @pl.when(j < steps)
    def _():
        part = all_ref.at[pl.ds(pl.multiple_of(j * deep, deep), deep), :]
        pltpu.make_async_copy(part, part, sems.at[j]).wait()
        w = part[...]
        w_ref[...] = w
        acc_ref[...] += dot(a_ref[...], w)

    @pl.when(j >= steps)
    def _():
        block = out_ref.shape[0]
        n1 = hat1_ref[...] * g1_ref[...] + s1_ref[...]
        mlp = acc_ref[pl.ds(pl.multiple_of((j - steps) * block, block), block), :]
        h = n1 + (mlp + b_ref[...])
        center = h - jnp.mean(h, axis=-1, keepdims=True)
        rstd = lax.rsqrt(jnp.mean(center * center, axis=-1, keepdims=True) + EPS)
        hat = center * rstd
        out_ref[...] = (hat * g2_ref[...] + s2_ref[...]).astype(BF16)
        cot = cot_ref[...].astype(F32)
        wide = cot * g2_ref[...]
        mean_a = jnp.mean(wide, axis=-1, keepdims=True)
        mean_b = jnp.mean(wide * hat, axis=-1, keepdims=True)
        dh = rstd * (wide - mean_a - hat * mean_b)
        dh_ref[...] = dh
        dm = dh.astype(BF16)
        dm_ref[...] = dm
        dg_ref[...] += jnp.sum(cot * hat, axis=0, keepdims=True)
        ds_ref[...] += jnp.sum(cot, axis=0, keepdims=True)
        db_ref[...] += jnp.sum(dm.astype(F32), axis=0, keepdims=True)


def down_norm(me, pieces, act, bias, hat1, g1, s1, g2, s2, cot, block=256, steps=4):
    rows, width = hat1.shape
    deep = act.shape[1]
    vec = full_spec((1, width))
    row = pl.BlockSpec((block, width), lambda j: (jnp.maximum(j - steps, 0), 0))
    return pl.pallas_call(
        functools.partial(down_norm_kernel, steps=steps),
        grid=(steps + rows // block,),
        in_specs=[SCALAR]
        + [pl.BlockSpec(memory_space=pl.ANY)] * 4
        + [pl.BlockSpec((rows, deep // steps), lambda j: (0, jnp.minimum(j, steps - 1)))]
        + [vec, row, vec, vec, vec, vec, row],
        out_specs=[row, row, row, vec, vec, vec]
        + [pl.BlockSpec((deep // steps, width), lambda j: (jnp.minimum(j, steps - 1), 0))],
        out_shape=[
            jax.ShapeDtypeStruct((rows, width), BF16),
            jax.ShapeDtypeStruct((rows, width), F32),
            jax.ShapeDtypeStruct((rows, width), BF16),
        ]
        + [jax.ShapeDtypeStruct((1, width), F32)] * 3
        + [jax.ShapeDtypeStruct((deep, width), BF16)],
        scratch_shapes=[
            pltpu.VMEM((deep, width), BF16),
            pltpu.VMEM((rows, width), F32),
            pltpu.SemaphoreType.DMA((steps,)),
        ],
        compiler_params=params(),
        cost_estimate=cost(2 * rows * width * deep, 2 * deep * (rows + width) + 14 * rows * width),
        name="down_norm",
    )(me, *pieces, act, bias, hat1, g1, s1, g2, s2, cot)


def split(value, core, chunk, keep_ref, send_ref):
    value = value.astype(BF16).reshape(-1, 2, 2, chunk // 2, value.shape[1])
    for half in range(2):
        even = value[:, 0, half].reshape(keep_ref.shape[1:])
        odd = value[:, 1, half].reshape(keep_ref.shape[1:])
        keep_ref[half] = jnp.where(core == 0, even, odd)
        send_ref[half] = jnp.where(core == 0, odd, even)


def join(keep, send, chunk):
    cols = keep.shape[-1]
    pair = [v.reshape(2, -1, chunk // 2, cols) for v in (keep, send)]
    return jnp.stack(pair, axis=0).transpose(2, 0, 1, 3, 4).reshape(-1, cols)


def down_grad_kernel(core_ref, a_ref, b_ref, keep_ref, send_ref):
    chunk = keep_ref.shape[1]
    split(t_dot(a_ref[...], b_ref[...]), core_ref[0], chunk, keep_ref, send_ref)


def down_grad(core, a, b):
    rows, deep = a.shape
    cols = b.shape[1]
    block = 4 * deep // CHUNKS
    out = pl.BlockSpec((2, block // 4, cols), lambda j: (0, j, 0))
    return pl.pallas_call(
        down_grad_kernel,
        grid=(deep // block,),
        in_specs=[SCALAR, pl.BlockSpec((rows, block), lambda j: (0, j)), full_spec((rows, cols))],
        out_specs=[out, out],
        out_shape=[jax.ShapeDtypeStruct((2, deep // 4, cols), BF16)] * 2,
        compiler_params=params(),
        cost_estimate=cost(2 * rows * deep * cols, 2 * (rows * deep + rows * cols + deep * cols)),
        name="down_grad",
    )(core, a, b)


def attn_grad_kernel(core_ref, xt_ref, *refs, n_parts, more):
    parts, rest = refs[:n_parts], refs[n_parts:]
    keep_ref, send_ref = rest[-2:]
    chunk = 32
    at = 0

    def put(value):
        nonlocal at
        cols = value.shape[1]
        here = [ref.at[:, :, at : at + cols] for ref in (keep_ref, send_ref)]
        split(value, core_ref[0], chunk, *here)
        at += cols

    for ref in parts:
        put(dot(xt_ref[...], ref[...]))
    if more == "out":
        put(t_dot(rest[0][...], rest[1][...]))
    else:
        put(rest[0][...])


def attn_grad(core, xt, parts, extra, more, block=256):
    width, rows = xt.shape
    in_specs = [SCALAR, row_spec(block, rows)] + [full_spec(p.shape) for p in parts]
    cols = sum(p.shape[1] for p in parts)
    if more == "out":
        in_specs += [pl.BlockSpec((rows, block), lambda i: (0, i)), full_spec(extra[1].shape)]
        cols += extra[1].shape[1]
    else:
        in_specs += [row_spec(block, extra[0].shape[1])]
        cols += extra[0].shape[1]
    out = pl.BlockSpec((2, block // 4, cols), lambda i: (0, i, 0))
    return pl.pallas_call(
        functools.partial(attn_grad_kernel, n_parts=len(parts), more=more),
        grid=(width // block,),
        in_specs=in_specs,
        out_specs=[out, out],
        out_shape=[jax.ShapeDtypeStruct((2, width // 4, cols), BF16)] * 2,
        compiler_params=params(),
        cost_estimate=cost(2 * rows * width * cols, 2 * (rows * width + cols * (rows + width))),
        name="attn_grad",
    )(core, xt, *parts, *extra)


def up_back_kernel(
    core_ref, dm_ref, w_ref, slope_ref, x_ref, du_ref, keep_ref, send_ref, db_ref, xt_ref
):
    @pl.when(pl.program_id(0) == 0)
    def _():
        xt_ref[...] = x_ref[...].T

    du = (dot_t(dm_ref[...], w_ref[...]) * slope_ref[...].astype(F32)).astype(BF16)
    du_ref[...] = du
    db_ref[...] = jnp.sum(du.astype(F32), axis=0, keepdims=True)
    split(dot(xt_ref[...], du), core_ref[0], xt_ref.shape[0] // CHUNKS, keep_ref, send_ref)


def up_back(core, dm, w_down, slope, x):
    rows, width = dm.shape
    deep = slope.shape[1]
    block = 4 * deep // CHUNKS
    col = pl.BlockSpec((rows, block), lambda j: (0, j))
    half = pl.BlockSpec((2, width // 4, block), lambda j: (0, 0, j))
    return pl.pallas_call(
        up_back_kernel,
        grid=(deep // block,),
        in_specs=[
            SCALAR,
            full_spec((rows, width)),
            pl.BlockSpec((block, width), lambda j: (j, 0)),
            col,
            full_spec((rows, width)),
        ],
        out_specs=[col, half, half, pl.BlockSpec((1, block), lambda j: (0, j))],
        out_shape=[
            jax.ShapeDtypeStruct((rows, deep), BF16),
            jax.ShapeDtypeStruct((2, width // 4, deep), BF16),
            jax.ShapeDtypeStruct((2, width // 4, deep), BF16),
            jax.ShapeDtypeStruct((1, deep), F32),
        ],
        scratch_shapes=[pltpu.VMEM((width, rows), BF16)],
        compiler_params=params(),
        cost_estimate=cost(4 * rows * width * deep, 4 * deep * (rows + width) + 4 * rows * width),
        name="up_back",
    )(core, dm, w_down, slope, x)


def norm_back_kernel(
    du_ref, w_ref, out_ref, dh2_ref, hat_ref, rstd_ref, g_ref,
    dh_ref, da_ref, dc_ref, dg_ref, ds_ref, db_ref,
):
    width = dh2_ref.shape[1]
    dn = dh2_ref[...]
    size = width // CHUNKS
    for j in range(du_ref.shape[1] // width):
        w = w_ref[:, j * size : (j + 1) * size, :].reshape(width, width)
        dn = dn + dot_t(du_ref[:, j * width : (j + 1) * width], w)
    hat = hat_ref[...]
    wide = dn * g_ref[...]
    mean_a = jnp.mean(wide, axis=-1, keepdims=True)
    mean_b = jnp.mean(wide * hat, axis=-1, keepdims=True)
    dh = rstd_ref[...] * (wide - mean_a - hat * mean_b)
    dh_ref[...] = dh
    da = dh.astype(BF16)
    da_ref[...] = da
    dc_ref[...] = dot_t(da, out_ref[...].reshape(width, width)).astype(BF16)

    @pl.when(pl.program_id(0) == 0)
    def _():
        dg_ref[...] = jnp.zeros_like(dg_ref)
        ds_ref[...] = jnp.zeros_like(ds_ref)
        db_ref[...] = jnp.zeros_like(db_ref)

    dg_ref[...] += jnp.sum(dn * hat, axis=0, keepdims=True)
    ds_ref[...] += jnp.sum(dn, axis=0, keepdims=True)
    db_ref[...] += jnp.sum(da.astype(F32), axis=0, keepdims=True)


def norm_back(du, held, dh2, hat, rstd, gain, block=256):
    rows, width = hat.shape
    deep = du.shape[1]
    vec = full_spec((1, width))
    row = row_spec(block, width)
    return pl.pallas_call(
        norm_back_kernel,
        grid=(rows // block,),
        in_specs=[row_spec(block, deep), up_weight(held), out_weight(held)]
        + [row, row, row_spec(block, 1), vec],
        out_specs=[row, row, row, vec, vec, vec],
        out_shape=[
            jax.ShapeDtypeStruct((rows, width), F32),
            jax.ShapeDtypeStruct((rows, width), BF16),
            jax.ShapeDtypeStruct((rows, width), BF16),
        ]
        + [jax.ShapeDtypeStruct((1, width), F32)] * 3,
        compiler_params=params(),
        cost_estimate=cost(2 * rows * width * deep, 2 * deep * (rows + width) + 14 * rows * width),
        name="norm_back",
    )(du, held, held, dh2, hat, rstd, gain)


def input_back_kernel(*refs):
    *parts, w_ref, dh_ref, o_ref = refs
    width = o_ref.shape[1]
    total = dh_ref[...]
    for which in range(3):
        pieces = [
            ref[:, at : at + 128]
            for ref in parts
            for at in range(which * 128, ref.shape[1], 384)
        ]
        col = which * width
        total = total + dot_t(jnp.concatenate(pieces, axis=1), w_ref[:, col : col + width])
    o_ref[...] = total.astype(BF16)


def input_back(parts, w, dh, block=256):
    rows, width = dh.shape
    return pl.pallas_call(
        input_back_kernel,
        grid=(rows // block,),
        in_specs=[row_spec(block, p.shape[1]) for p in parts]
        + [pl.BlockSpec((width, 3 * width), lambda i: (0, 0)), row_spec(block, width)],
        out_specs=row_spec(block, width),
        out_shape=jax.ShapeDtypeStruct((rows, width), BF16),
        compiler_params=params(),
        cost_estimate=cost(6 * rows * width * width, 18 * rows * width),
        name="input_back",
    )(*parts, w, dh)


def exchange(x, n, mask):
    return lax.ppermute(x, "dp", [(i, i ^ mask) for i in range(n)])


def pick(x, axis, index):
    return lax.dynamic_index_in_dim(x, index, axis, keepdims=False)


def tie(*values):
    return lax.optimization_barrier(values)


class Scatter:
    def __init__(self, keep, send, n, r):
        self.n, self.h, self.me, self.cols = n, r // 2, lax.axis_index("dp"), keep.shape[-1]
        self.keep, self.got = keep, exchange(send, n, 1)
        self.left = [[4, 3, 2, 1], [4, 3, 2, 1]]
        self.step = 0

    def part(self, side, bit, which):
        left = self.left[side]
        at, size = left.index(bit), 1 << len(left)
        shape = (1 << at, 2, size >> (at + 1), self.h, self.cols)
        total = None
        for value in self.held[side]:
            lead = value.size // math.prod(shape)
            value = value.reshape(lead, *shape)
            start = (side if lead == 2 else 0, 0, which, 0, 0, 0)
            value = lax.dynamic_slice(value, start, (1, shape[0], 1, *shape[2:])).astype(F32)
            total = value if total is None else total + value
        return total.reshape(size // 2, self.h, self.cols)

    def behind(self, along):
        if self.step == 0:
            flat = tie(self.keep, self.got, *along)
            self.held = [flat[:2]] * 2
            return flat[2:]
        flat = tie(*self.held[0], *self.held[1], *along)
        self.held = [flat[:2], flat[2:4]]
        return flat[4:]

    def halve(self, *along):
        along = self.behind(along)
        bits = ((2, 1), (1, 2))
        sums = []
        for side in range(2):
            bit = bits[side][self.step]
            mine = (self.me >> bit) & 1
            sums += [self.part(side, bit, which).astype(BF16) for which in (1 - mine, mine)]
        *sums, = tie(*sums, *along)
        sums, along = sums[:4], sums[4:]
        for side in range(2):
            bit = bits[side][self.step]
            self.held[side] = (sums[2 * side + 1], exchange(sums[2 * side], self.n, 1 << bit))
            self.left[side].remove(bit)
        self.step += 1
        return along[0] if len(along) == 1 else along

    def column_one(self, *along):
        along = self.behind(along)
        mine = self.me >> 4
        sent, kept = [
            jnp.concatenate([self.part(side, 4, which) for side in range(2)], axis=1).astype(BF16)
            for which in (1 - mine, mine)
        ]
        sent, kept, *along = tie(sent, kept, *along)
        self.pair = (kept, exchange(sent, self.n, 16))
        return along[0] if len(along) == 1 else along

    def column_two(self, *along):
        *self.pair, = tie(*self.pair, *along)
        self.pair, along = self.pair[:2], self.pair[2:]
        mine = (self.me >> 3) & 1
        sent, kept = [
            sum(pick(value, 0, which).astype(F32) for value in self.pair) for which in (1 - mine, mine)
        ]
        sent, kept, *along = tie(sent.astype(BF16), kept, *along)
        self.last = [kept, exchange(sent, self.n, 8)]
        return along[0] if len(along) == 1 else along

    def column(self, *along):
        along = self.behind(along)
        mine = self.me >> 3
        sums = [
            jnp.concatenate(
                [
                    sum(pick(v, 0, mine ^ k).astype(F32) for v in self.held[side])
                    for side in range(2)
                ],
                axis=0,
            )
            for k in range(4)
        ]
        *sums, = tie(sums[0], *[v.astype(BF16) for v in sums[1:]], *along)
        sums, along = sums[:4], sums[4:]
        self.last = sums[:1] + [exchange(sums[k], self.n, k << 3) for k in (1, 2, 3)]
        return along[0] if len(along) == 1 else along

    def after(self, *along):
        flat = tie(*self.last, *along)
        self.last, along = flat[: len(self.last)], flat[len(self.last) :]
        return along[0] if len(along) == 1 else along

    def result(self):
        return sum(value.astype(F32) for value in self.last)


class PlainScatter:
    def __init__(self, keep, send, n, r):
        self.keep = keep
        whole = join(keep, send, keep.shape[1] * 4 // CHUNKS)
        self.total = lax.psum_scatter(whole.astype(F32), "dp", scatter_dimension=0, tiled=True)

    def halve(self, *along):
        return along[0] if len(along) == 1 else along

    column = column_one = column_two = after = halve

    def result(self):
        return self.total


def gather(x):
    return lax.all_gather(x, "dp", axis=0, tiled=True)


class Gather:
    def __init__(self, x, n):
        self.n, self.shape = n, x.shape
        self.near = [x] + [exchange(x, n, k << 3) for k in (1, 2, 3)]

    def after(self, *along):
        flat = tie(*self.near, *along)
        self.near = flat[: len(self.near)]
        along = flat[len(self.near) :]
        return along[0] if len(along) == 1 else along

    def column(self, *along):
        h = self.shape[0] // 2
        sides = [jnp.concatenate([v[at : at + h] for v in self.near], axis=0) for at in (0, h)]
        *sides, = tie(*sides, *along)
        self.near = [sides[0], exchange(sides[0], self.n, 2), sides[1], exchange(sides[1], self.n, 4)]
        along = sides[2:]
        return along[0] if len(along) == 1 else along

    def join(self):
        return [jnp.concatenate(self.near[k : k + 2], axis=0) for k in (0, 2)]

    def plane(self, *along):
        sides = self.join()
        *sides, = tie(*sides, *along)
        self.near = [sides[0], exchange(sides[0], self.n, 4), sides[1], exchange(sides[1], self.n, 2)]
        along = sides[2:]
        return along[0] if len(along) == 1 else along

    def pair(self, *along):
        sides = self.join()
        *sides, = tie(*sides, *along)
        pieces = sides[:2] + [exchange(v, self.n, 1) for v in sides[:2]]
        pieces = [v.reshape(16, self.shape[0] // 2, self.shape[1]) for v in pieces]
        return pieces, *sides[2:]


def plain_pieces(whole, size):
    chips = whole.reshape(4, 2, 2, 2, 2, size // 2, whole.shape[1])
    upper = chips[:, :, :, :, 0].transpose(3, 1, 2, 0, 4, 5)
    lower = chips[:, :, :, :, 1].transpose(3, 2, 1, 0, 4, 5)
    return [v[core].reshape(16, size // 2, -1) for core in range(2) for v in (upper, lower)]


def columns(vector, r):
    return vector.reshape(-1, r).T


def table_of(vectors, n, r):
    parts = [v.reshape(n, -1, r).transpose(0, 2, 1).reshape(n * r, -1) for v in vectors]
    return jnp.concatenate(parts, axis=1)


def local(
    n,
    tokens,
    cotangent,
    w_qkv,
    q_bias,
    v_bias,
    w_out,
    out_bias,
    attn_gain,
    attn_shift,
    w_up,
    up_bias,
    w_down,
    down_bias,
    mlp_gain,
    mlp_shift,
):
    rows, width = tokens.shape
    r = w_qkv.shape[0]
    wide = w_up.shape[1] // width
    vectors = (
        q_bias, v_bias, out_bias, attn_gain, attn_shift, down_bias, mlp_gain, mlp_shift, up_bias,
    )
    small = jnp.concatenate([columns(v, r) for v in vectors], axis=1)
    small = jnp.pad(small, ((0, 0), (0, 128 - small.shape[1])))
    first = jnp.concatenate([w_qkv, small], axis=1)
    tokens_t = tokens.T
    core, me, pairs = jnp.int32(0), jnp.int32(0), width // 128
    if n == CHUNKS:
        scatter, me = Scatter, lax.axis_index("dp")
        core = me & 1
        blocks = [w_up[:, j * width : (j + 1) * width] for j in range(wide)]
        others = jnp.concatenate(blocks + [w_out], axis=0)
        first = Gather(first, n)
        others = first.after(others)
        first.column()
        held = gather(others).reshape(CHUNKS, -1, width)
        first.plane()
        pieces, tokens_t, w_down_share = first.pair(tokens_t, w_down)
        second = Gather(w_down_share, n)
    else:
        scatter = PlainScatter
        up = gather(w_up).reshape(CHUNKS, width // CHUNKS, wide, width).transpose(0, 2, 1, 3)
        up = up.reshape(CHUNKS, wide * width // CHUNKS, width)
        out = gather(w_out).reshape(CHUNKS, width // CHUNKS, width)
        held = jnp.concatenate([up, out], axis=1)
        pieces = plain_pieces(gather(first), width // CHUNKS)
        down_pieces = plain_pieces(gather(w_down), wide * width // CHUNKS)
    core, me = core.reshape(1), me.reshape(1)

    qkv, w_full, table = project(me, tokens, pieces)
    ob, g1, s1, db, g2, s2 = [table[j : j + 1] for j in range(2, 8)]
    ub = table[8 : 8 + wide].reshape(wide, CHUNKS, -1).transpose(1, 0, 2).reshape(1, -1)
    half = pairs // 2
    ctx, lse = attend(qkv, width, 0, half)
    if n == CHUNKS:
        ctx = second.column(second.after(ctx))
    ctx, lse = attend(qkv, width, half, pairs - half, (ctx, lse))
    if n == CHUNKS:
        ctx = second.plane(second.after(ctx))
    hat1, rstd1, n1_low = out_norm(ctx, held, ob, tokens, g1, s1)
    act, slope = up_gelu(n1_low, held, ub, 0)
    if n == CHUNKS:
        down_pieces, act = second.pair(second.after(act))
    act, slope = up_gelu(n1_low, held, ub, 1, (act, slope))
    layer_out, dh2, dm, d_g2, d_s2, d_db, full_down = down_norm(
        me, down_pieces, act, db, hat1, g1, s1, g2, s2, cotangent
    )

    sums = {}

    def at(name, *along):
        for who, step in PLAN[name]:
            along = getattr(sums[who], step)(*along)
            along = along if type(along) in (tuple, list) else (along,)
        return along

    def back(k):
        return attend_back(qkv, ctx, dctx, lse, width, sum(PARTS[:k]), PARTS[k])

    sums["D"] = scatter(*down_grad(core, act, dm), n, w_down.shape[0])
    du, keep, send, d_ub = up_back(core, dm, full_down, slope, n1_low)
    sums["U"] = scatter(keep, send, n, r)
    (du,) = at("up_back", du)
    dh1, da, dctx, d_g1, d_s1, d_ob = norm_back(du, held, dh2, hat1, rstd1, g1)
    (dctx,) = at("norm_back", dctx)
    first, sq0, sv0 = back(0)
    (first,) = at("first", first)
    keep, send = attn_grad(core, tokens_t, [first], [ctx, da], "out")
    sums["E"] = scatter(keep, send, n, r)
    keep, dctx = at("early", sums["E"].keep, dctx)
    sums["E"].keep = keep
    second, sq1, sv1 = back(1)
    second, dctx = at("second", second, dctx)
    third, sq2, sv2 = back(2)
    (third,) = at("third", third)
    d_qb = jnp.concatenate([sq0, sq1, sq2], axis=1)
    d_vb = jnp.concatenate([sv0, sv1, sv2], axis=1)
    d_small = table_of([d_qb, d_vb, d_ob, d_g1, d_s1, d_db, d_g2, d_s2, d_ub], CHUNKS, width // CHUNKS)
    d_small = jnp.pad(d_small, ((0, 0), (0, 128 - d_small.shape[1]))).astype(BF16)
    keep, send = attn_grad(core, tokens_t, [second, third], [d_small], "small")
    sums["L"] = scatter(keep, send, n, r)
    keep, dh1 = at("late", sums["L"].keep, dh1)
    sums["L"].keep = keep
    input_grad = input_back([first, second, third], w_full, dh1)
    (input_grad,) = at("input_back", input_grad)
    down_sum, up_sum, early_sum, late_sum = [sums[k] for k in "DUEL"]

    early, late = early_sum.result(), late_sum.result()
    qkv_cols = PARTS[0] * 384
    d_qkv = jnp.concatenate([early[:, :qkv_cols], late[:, : 3 * width - qkv_cols]], axis=1)
    d_qkv = d_qkv.reshape(r, pairs, 3, 128).transpose(0, 2, 1, 3).reshape(r, 3 * width)
    d_out = early[:, qkv_cols:]
    d_small = late[:, 3 * width - qkv_cols :]

    def vector(start, k=1):
        return d_small[:, start : start + k].T.reshape(-1)

    d_qb, d_vb, d_ob, d_g1, d_s1, d_db, d_g2, d_s2 = [vector(j) for j in range(8)]
    d_ub = d_small[:, 8 : 8 + wide]
    d_ub = d_ub.T.reshape(-1)
    return (
        layer_out, input_grad, d_qkv, d_qb, d_vb, d_out, d_ob, d_g1, d_s1,
        up_sum.result(), d_ub, down_sum.result(), d_db, d_g2, d_s2,
    )


def solution(mesh):
    flat, square = P("dp"), P("dp", None)
    in_specs = (
        square, square, square, flat, flat, square, flat, flat, flat,
        square, flat, square, flat, flat, flat,
    )
    return jax.shard_map(
        functools.partial(local, mesh.shape["dp"]),
        mesh=mesh,
        in_specs=in_specs,
        out_specs=in_specs,
        check_vma=False,
    )
```

```python
import functools
import math

import jax
import jax.numpy as jnp
from jax import lax
from jax.experimental import pallas as pl
from jax.experimental.pallas import tpu as pltpu
from jax.sharding import PartitionSpec as P

HD = 64
LEN = 512
EPS = 1e-05
CHUNKS = 32
F32 = jnp.float32
BF16 = jnp.bfloat16
MIB = 1 << 20


def params(limit=48):
    return pltpu.CompilerParams(vmem_limit_bytes=limit * MIB)


COST = 0.02
PARTS = (3, 3, 2)
PLAN = {
    "up_back": [("D", "halve")],
    "norm_back": [("D", "halve"), ("U", "halve")],
    "first": [],
    "early": [("D", "column"), ("U", "halve")],
    "second": [("E", "halve")],
    "third": [("D", "after"), ("U", "column")],
    "late": [("E", "halve"), ("L", "halve"), ("U", "after")],
    "input_back": [("L", "halve"), ("E", "column"), ("L", "column")],
}


def cost(flops, nbytes, trans=0):
    return pl.CostEstimate(
        flops=int(COST * flops), bytes_accessed=int(COST * nbytes), transcendentals=int(COST * trans)
    )


def dot(a, b):
    return jnp.dot(a, b, preferred_element_type=F32)


def dot_t(a, b):
    return lax.dot_general(a, b, (((1,), (1,)), ((), ())), preferred_element_type=F32)


def t_dot(a, b):
    return lax.dot_general(a, b, (((0,), (0,)), ((), ())), preferred_element_type=F32)


SCALAR = pl.BlockSpec(memory_space=pltpu.SMEM)


def row_spec(block, width):
    return pl.BlockSpec((block, width), lambda i: (i, 0))


def full_spec(shape):
    return pl.BlockSpec(shape, lambda i: (0,) * len(shape))


def place(me, pieces, out_ref, sem_of):
    size = out_ref.shape[0] // CHUNKS
    h = size // 2
    for device in range(CHUNKS):
        mask = jnp.bitwise_xor(me, device)
        x, y, z = (mask >> 1) & 1, (mask >> 2) & 1, mask >> 3
        for side in range(2):
            k = ((x << 3 | y << 2) if side else (y << 3 | x << 2)) | z
            target = out_ref.at[pl.ds(device * size + side * h, h), :]
            for core in range(2):

                @pl.when(mask & 1 == core)
                def _():
                    piece = pieces[2 * core + side].at[k]
                    pltpu.make_async_copy(piece, target, sem_of(device)).start()


def project_kernel(me_ref, x_ref, *refs):
    pieces, (o_ref, w_ref, t_ref, sem) = refs[:4], refs[4:]
    j = pl.program_id(0)
    block = o_ref.shape[1]
    width = x_ref.shape[1]

    @pl.when(j == 0)
    def _():
        place(me_ref[0], pieces, w_ref, lambda device: sem)
        pltpu.make_async_copy(w_ref, w_ref, sem).wait()
        table = w_ref[:, 3 * width :].astype(F32).T
        t_ref[...] = table[: t_ref.shape[0]]

    per = width // block
    at = pl.multiple_of((j % per) * block, block)
    bias = jnp.where(
        j < per,
        t_ref[0:1, pl.ds(at, block)],
        jnp.where(j >= 2 * per, t_ref[1:2, pl.ds(at, block)], 0.0),
    )
    w = w_ref[:, pl.ds(pl.multiple_of(j * block, block), block)]
    o_ref[...] = (dot(x_ref[...], w) + bias).astype(BF16)


def project(me, x, pieces, block=1024):
    rows, width = x.shape
    cols = 3 * width
    held = pieces[0].shape[2]
    return pl.pallas_call(
        project_kernel,
        grid=(cols // block,),
        in_specs=[SCALAR, full_spec((rows, width))] + [pl.BlockSpec(memory_space=pl.ANY)] * 4,
        out_specs=[
            pl.BlockSpec((rows, block), lambda j: (0, j)),
            full_spec((width, held)),
            full_spec((16, width)),
        ],
        out_shape=[
            jax.ShapeDtypeStruct((rows, cols), BF16),
            jax.ShapeDtypeStruct((width, held), BF16),
            jax.ShapeDtypeStruct((16, width), F32),
        ],
        scratch_shapes=[pltpu.SemaphoreType.DMA],
        compiler_params=params(),
        cost_estimate=cost(2 * rows * width * cols, 2 * (rows * width + 2 * width * cols + rows * cols)),
        name="project",
    )(me, x, *pieces)


def head_mask(shape, h):
    lane = lax.broadcasted_iota(jnp.int32, shape, 1)
    return (lane >= h * HD) & (lane < (h + 1) * HD)


def attend_kernel(q_ref, k_ref, v_ref, *refs):
    ctx_ref, lse_ref = refs[-2:]
    q = q_ref[...] * jnp.asarray(1.0 / math.sqrt(HD), BF16)
    k = k_ref[...]
    vt = v_ref[...].T
    parts = []
    for h in range(2):
        qh = jnp.where(head_mask(q.shape, h), q, jnp.zeros_like(q))
        s = dot_t(k, qh)
        m = jnp.max(s, axis=0, keepdims=True)
        e = jnp.exp(s - m)
        total = jnp.sum(e, axis=0, keepdims=True)
        c = dot(vt[h * HD : (h + 1) * HD, :], e.astype(BF16))
        parts.append(c * (1.0 / total))
        lse_ref[0, 0, h : h + 1, :] = m + jnp.log(total)
    ctx_ref[...] = jnp.concatenate(parts, axis=0).T.astype(BF16)


def attend(qkv, width, start, n_pairs, held=()):
    rows = qkv.shape[0]
    count, pairs = rows // LEN, width // 128
    return pl.pallas_call(
        attend_kernel,
        grid=(n_pairs, count),
        in_specs=[
            pl.BlockSpec((LEN, 128), lambda p, s: (s, start + p)),
            pl.BlockSpec((LEN, 128), lambda p, s: (s, pairs + start + p)),
            pl.BlockSpec((LEN, 128), lambda p, s: (s, 2 * pairs + start + p)),
        ]
        + [pl.BlockSpec(memory_space=pl.ANY)] * len(held),
        out_specs=[
            pl.BlockSpec((LEN, 128), lambda p, s: (s, start + p)),
            pl.BlockSpec((1, 1, 2, LEN), lambda p, s: (start + p, s, 0, 0)),
        ],
        out_shape=[
            jax.ShapeDtypeStruct((rows, width), BF16),
            jax.ShapeDtypeStruct((pairs, count, 2, LEN), F32),
        ],
        input_output_aliases={3 + k: k for k in range(len(held))},
        compiler_params=params(),
        cost_estimate=cost(
            rows * n_pairs * LEN * 2048, 1024 * rows * n_pairs, rows * n_pairs * LEN * 2
        ),
        name="attend",
    )(qkv, qkv, qkv, *held)


def attend_back_kernel(q_ref, k_ref, v_ref, c_ref, d_ref, lse_ref, dp_ref, sq_ref, sv_ref):
    scale = 1.0 / math.sqrt(HD)
    q = q_ref[...] * jnp.asarray(scale, BF16)
    k = k_ref[...]
    v = v_ref[...]
    d = d_ref[...]
    kt = k.T
    prod = (d.astype(F32) * c_ref[...].astype(F32)).T
    dk = dv = None
    parts = []
    for h in range(2):
        mask = head_mask(q.shape, h)
        qh = jnp.where(mask, q, jnp.zeros_like(q))
        dh = jnp.where(mask, d, jnp.zeros_like(d))
        delta = jnp.sum(prod[h * HD : (h + 1) * HD, :], axis=0, keepdims=True)
        p = jnp.exp(dot_t(k, qh) - lse_ref[0, 0, h : h + 1, :])
        ds = (p * (dot_t(v, dh) - delta)).astype(BF16)
        dv_h = dot(p.astype(BF16), dh)
        dk_h = dot(ds, qh)
        dv = dv_h if dv is None else dv + dv_h
        dk = dk_h if dk is None else dk + dk_h
        parts.append(dot(kt[h * HD : (h + 1) * HD, :], ds) * scale)
    dq = jnp.concatenate(parts, axis=0).T.astype(BF16)
    dv = dv.astype(BF16)
    dp_ref[:, 0:128] = dq
    dp_ref[:, 128:256] = dk.astype(BF16)
    dp_ref[:, 256:384] = dv
    sq = jnp.sum(dq.astype(F32), axis=0, keepdims=True)
    sv = jnp.sum(dv.astype(F32), axis=0, keepdims=True)
    first = pl.program_id(1) == 0

    @pl.when(first)
    def _():
        sq_ref[...] = sq
        sv_ref[...] = sv

    @pl.when(jnp.logical_not(first))
    def _():
        sq_ref[...] += sq
        sv_ref[...] += sv


def attend_back(qkv, ctx, dctx, lse, width, start, n_pairs):
    rows = qkv.shape[0]
    count, pairs = rows // LEN, width // 128
    cols = n_pairs * 128
    sum_block = pl.BlockSpec((1, 128), lambda p, s: (0, p))
    return pl.pallas_call(
        attend_back_kernel,
        grid=(n_pairs, count),
        in_specs=[
            pl.BlockSpec((LEN, 128), lambda p, s: (s, start + p)),
            pl.BlockSpec((LEN, 128), lambda p, s: (s, pairs + start + p)),
            pl.BlockSpec((LEN, 128), lambda p, s: (s, 2 * pairs + start + p)),
            pl.BlockSpec((LEN, 128), lambda p, s: (s, start + p)),
            pl.BlockSpec((LEN, 128), lambda p, s: (s, start + p)),
            pl.BlockSpec((1, 1, 2, LEN), lambda p, s: (start + p, s, 0, 0)),
        ],
        out_specs=[pl.BlockSpec((LEN, 384), lambda p, s: (s, p)), sum_block, sum_block],
        out_shape=[jax.ShapeDtypeStruct((rows, 3 * cols), BF16)]
        + [jax.ShapeDtypeStruct((1, cols), F32)] * 2,
        compiler_params=params(),
        cost_estimate=cost(rows * cols * LEN * 10 * 4, 16 * rows * cols, rows * cols * LEN // HD),
        name="attend_back",
    )(qkv, qkv, qkv, ctx, dctx, lse)


def out_weight(held):
    _, rows, width = held.shape
    size = width // CHUNKS
    return pl.BlockSpec((CHUNKS, size, width), lambda i: (0, rows // size - 1, 0))


def up_weight(held):
    _, rows, width = held.shape
    return pl.BlockSpec((CHUNKS, rows - width // CHUNKS, width), lambda i: (0, 0, 0))


def out_norm_kernel(c_ref, w_ref, b_ref, x_ref, g_ref, s_ref, hat_ref, rstd_ref, low_ref):
    w = w_ref[...].reshape(-1, x_ref.shape[1])
    h = x_ref[...].astype(F32) + (dot(c_ref[...], w) + b_ref[...])
    center = h - jnp.mean(h, axis=-1, keepdims=True)
    rstd = lax.rsqrt(jnp.mean(center * center, axis=-1, keepdims=True) + EPS)
    hat = center * rstd
    hat_ref[...] = hat
    rstd_ref[...] = rstd
    low_ref[...] = (hat * g_ref[...] + s_ref[...]).astype(BF16)


def out_norm(ctx, held, bias, tokens, gain, shift, block=256):
    rows, width = tokens.shape
    vec = full_spec((1, width))
    return pl.pallas_call(
        out_norm_kernel,
        grid=(rows // block,),
        in_specs=[
            row_spec(block, width),
            out_weight(held),
            vec,
            row_spec(block, width),
            vec,
            vec,
        ],
        out_specs=[row_spec(block, width), row_spec(block, 1), row_spec(block, width)],
        out_shape=[
            jax.ShapeDtypeStruct((rows, width), F32),
            jax.ShapeDtypeStruct((rows, 1), F32),
            jax.ShapeDtypeStruct((rows, width), BF16),
        ],
        compiler_params=params(),
        cost_estimate=cost(2 * rows * width * width, 14 * rows * width),
        name="out_norm",
    )(ctx, held, bias, tokens, gain, shift)


ERF_P = 0.3275911 / math.sqrt(2.0)
ERF_A = (0.254829592, -0.284496736, 1.421413741, -1.453152027, 1.061405429)


def gelu_pair(u):
    t = 1.0 / (1.0 + ERF_P * jnp.abs(u))
    e = jnp.exp(-0.5 * (u * u))
    poly = t * (ERF_A[0] + t * (ERF_A[1] + t * (ERF_A[2] + t * (ERF_A[3] + t * ERF_A[4]))))
    tail = 0.5 * poly * e
    cdf = jnp.where(u >= 0, 1.0 - tail, tail)
    return u * cdf, cdf + u * e * (1.0 / math.sqrt(2.0 * math.pi))


def up_kernel(x_ref, w_ref, b_ref, *refs):
    act_ref, slope_ref = refs[-2:]
    block = act_ref.shape[1]
    u = dot(x_ref[...], w_ref[...].reshape(-1, block)) + b_ref[...]
    act, slope = gelu_pair(u)
    act_ref[...] = act.astype(BF16)
    slope_ref[...] = slope.astype(BF16)


def up_gelu(x, held, bias, half, done=(), block=512):
    rows, width = x.shape
    cols = bias.shape[1]
    per, steps = width // block, cols // block // 2
    first = half * steps
    col = pl.BlockSpec((rows, block), lambda j: (0, first + j))
    return pl.pallas_call(
        up_kernel,
        grid=(steps,),
        in_specs=[
            full_spec((rows, width)),
            pl.BlockSpec((CHUNKS, width // CHUNKS, block), lambda j: (0, (first + j) // per, (first + j) % per)),
            pl.BlockSpec((1, block), lambda j: (0, first + j)),
        ]
        + [pl.BlockSpec(memory_space=pl.ANY)] * len(done),
        out_specs=[col, col],
        out_shape=[jax.ShapeDtypeStruct((rows, cols), BF16)] * 2,
        input_output_aliases={3 + k: k for k in range(len(done))},
        compiler_params=params(),
        cost_estimate=cost(
            rows * width * cols, width * cols + 2 * rows * cols, rows * cols
        ),
        name="up_gelu",
    )(x, held, bias, *done)


def down_norm_kernel(
    me_ref, p0_ref, p1_ref, p2_ref, p3_ref,
    a_ref, b_ref, hat1_ref, g1_ref, s1_ref, g2_ref, s2_ref, cot_ref,
    out_ref, dh_ref, dm_ref, dg_ref, ds_ref, db_ref, w_ref, all_ref, acc_ref, sems, *, steps,
):
    j = pl.program_id(0)
    deep = all_ref.shape[0] // steps

    @pl.when(j == 0)
    def _():
        pieces = (p0_ref, p1_ref, p2_ref, p3_ref)
        place(me_ref[0], pieces, all_ref, lambda device: sems.at[device * steps // CHUNKS])
        dg_ref[...] = jnp.zeros_like(dg_ref)
        ds_ref[...] = jnp.zeros_like(ds_ref)
        db_ref[...] = jnp.zeros_like(db_ref)
        acc_ref[...] = jnp.zeros_like(acc_ref)

    @pl.when(j < steps)
    def _():
        part = all_ref.at[pl.ds(pl.multiple_of(j * deep, deep), deep), :]
        pltpu.make_async_copy(part, part, sems.at[j]).wait()
        w = part[...]
        w_ref[...] = w
        acc_ref[...] += dot(a_ref[...], w)

    @pl.when(j >= steps)
    def _():
        block = out_ref.shape[0]
        n1 = hat1_ref[...] * g1_ref[...] + s1_ref[...]
        mlp = acc_ref[pl.ds(pl.multiple_of((j - steps) * block, block), block), :]
        h = n1 + (mlp + b_ref[...])
        center = h - jnp.mean(h, axis=-1, keepdims=True)
        rstd = lax.rsqrt(jnp.mean(center * center, axis=-1, keepdims=True) + EPS)
        hat = center * rstd
        out_ref[...] = (hat * g2_ref[...] + s2_ref[...]).astype(BF16)
        cot = cot_ref[...].astype(F32)
        wide = cot * g2_ref[...]
        mean_a = jnp.mean(wide, axis=-1, keepdims=True)
        mean_b = jnp.mean(wide * hat, axis=-1, keepdims=True)
        dh = rstd * (wide - mean_a - hat * mean_b)
        dh_ref[...] = dh
        dm = dh.astype(BF16)
        dm_ref[...] = dm
        dg_ref[...] += jnp.sum(cot * hat, axis=0, keepdims=True)
        ds_ref[...] += jnp.sum(cot, axis=0, keepdims=True)
        db_ref[...] += jnp.sum(dm.astype(F32), axis=0, keepdims=True)


def down_norm(me, pieces, act, bias, hat1, g1, s1, g2, s2, cot, block=256, steps=4):
    rows, width = hat1.shape
    deep = act.shape[1]
    vec = full_spec((1, width))
    row = pl.BlockSpec((block, width), lambda j: (jnp.maximum(j - steps, 0), 0))
    return pl.pallas_call(
        functools.partial(down_norm_kernel, steps=steps),
        grid=(steps + rows // block,),
        in_specs=[SCALAR]
        + [pl.BlockSpec(memory_space=pl.ANY)] * 4
        + [pl.BlockSpec((rows, deep // steps), lambda j: (0, jnp.minimum(j, steps - 1)))]
        + [vec, row, vec, vec, vec, vec, row],
        out_specs=[row, row, row, vec, vec, vec]
        + [pl.BlockSpec((deep // steps, width), lambda j: (jnp.minimum(j, steps - 1), 0))],
        out_shape=[
            jax.ShapeDtypeStruct((rows, width), BF16),
            jax.ShapeDtypeStruct((rows, width), F32),
            jax.ShapeDtypeStruct((rows, width), BF16),
        ]
        + [jax.ShapeDtypeStruct((1, width), F32)] * 3
        + [jax.ShapeDtypeStruct((deep, width), BF16)],
        scratch_shapes=[
            pltpu.VMEM((deep, width), BF16),
            pltpu.VMEM((rows, width), F32),
            pltpu.SemaphoreType.DMA((steps,)),
        ],
        compiler_params=params(),
        cost_estimate=cost(2 * rows * width * deep, 2 * deep * (rows + width) + 14 * rows * width),
        name="down_norm",
    )(me, *pieces, act, bias, hat1, g1, s1, g2, s2, cot)


def split(value, core, chunk, keep_ref, send_ref):
    value = value.astype(BF16).reshape(-1, 2, 2, chunk // 2, value.shape[1])
    for half in range(2):
        even = value[:, 0, half].reshape(keep_ref.shape[1:])
        odd = value[:, 1, half].reshape(keep_ref.shape[1:])
        keep_ref[half] = jnp.where(core == 0, even, odd)
        send_ref[half] = jnp.where(core == 0, odd, even)


def join(keep, send, chunk):
    cols = keep.shape[-1]
    pair = [v.reshape(2, -1, chunk // 2, cols) for v in (keep, send)]
    return jnp.stack(pair, axis=0).transpose(2, 0, 1, 3, 4).reshape(-1, cols)


def down_grad_kernel(core_ref, a_ref, b_ref, keep_ref, send_ref):
    chunk = keep_ref.shape[1]
    split(t_dot(a_ref[...], b_ref[...]), core_ref[0], chunk, keep_ref, send_ref)


def down_grad(core, a, b):
    rows, deep = a.shape
    cols = b.shape[1]
    block = 4 * deep // CHUNKS
    out = pl.BlockSpec((2, block // 4, cols), lambda j: (0, j, 0))
    return pl.pallas_call(
        down_grad_kernel,
        grid=(deep // block,),
        in_specs=[SCALAR, pl.BlockSpec((rows, block), lambda j: (0, j)), full_spec((rows, cols))],
        out_specs=[out, out],
        out_shape=[jax.ShapeDtypeStruct((2, deep // 4, cols), BF16)] * 2,
        compiler_params=params(),
        cost_estimate=cost(2 * rows * deep * cols, 2 * (rows * deep + rows * cols + deep * cols)),
        name="down_grad",
    )(core, a, b)


def attn_grad_kernel(core_ref, xt_ref, *refs, n_parts, more):
    parts, rest = refs[:n_parts], refs[n_parts:]
    keep_ref, send_ref = rest[-2:]
    chunk = 32
    at = 0

    def put(value):
        nonlocal at
        cols = value.shape[1]
        here = [ref.at[:, :, at : at + cols] for ref in (keep_ref, send_ref)]
        split(value, core_ref[0], chunk, *here)
        at += cols

    for ref in parts:
        put(dot(xt_ref[...], ref[...]))
    if more == "out":
        put(t_dot(rest[0][...], rest[1][...]))
    else:
        put(rest[0][...])


def attn_grad(core, xt, parts, extra, more, block=256):
    width, rows = xt.shape
    in_specs = [SCALAR, row_spec(block, rows)] + [full_spec(p.shape) for p in parts]
    cols = sum(p.shape[1] for p in parts)
    if more == "out":
        in_specs += [pl.BlockSpec((rows, block), lambda i: (0, i)), full_spec(extra[1].shape)]
        cols += extra[1].shape[1]
    else:
        in_specs += [row_spec(block, extra[0].shape[1])]
        cols += extra[0].shape[1]
    out = pl.BlockSpec((2, block // 4, cols), lambda i: (0, i, 0))
    return pl.pallas_call(
        functools.partial(attn_grad_kernel, n_parts=len(parts), more=more),
        grid=(width // block,),
        in_specs=in_specs,
        out_specs=[out, out],
        out_shape=[jax.ShapeDtypeStruct((2, width // 4, cols), BF16)] * 2,
        compiler_params=params(),
        cost_estimate=cost(2 * rows * width * cols, 2 * (rows * width + cols * (rows + width))),
        name="attn_grad",
    )(core, xt, *parts, *extra)


def up_back_kernel(
    core_ref, dm_ref, w_ref, slope_ref, x_ref, du_ref, keep_ref, send_ref, db_ref, xt_ref
):
    @pl.when(pl.program_id(0) == 0)
    def _():
        xt_ref[...] = x_ref[...].T

    du = (dot_t(dm_ref[...], w_ref[...]) * slope_ref[...].astype(F32)).astype(BF16)
    du_ref[...] = du
    db_ref[...] = jnp.sum(du.astype(F32), axis=0, keepdims=True)
    split(dot(xt_ref[...], du), core_ref[0], xt_ref.shape[0] // CHUNKS, keep_ref, send_ref)


def up_back(core, dm, w_down, slope, x):
    rows, width = dm.shape
    deep = slope.shape[1]
    block = 4 * deep // CHUNKS
    col = pl.BlockSpec((rows, block), lambda j: (0, j))
    half = pl.BlockSpec((2, width // 4, block), lambda j: (0, 0, j))
    return pl.pallas_call(
        up_back_kernel,
        grid=(deep // block,),
        in_specs=[
            SCALAR,
            full_spec((rows, width)),
            pl.BlockSpec((block, width), lambda j: (j, 0)),
            col,
            full_spec((rows, width)),
        ],
        out_specs=[col, half, half, pl.BlockSpec((1, block), lambda j: (0, j))],
        out_shape=[
            jax.ShapeDtypeStruct((rows, deep), BF16),
            jax.ShapeDtypeStruct((2, width // 4, deep), BF16),
            jax.ShapeDtypeStruct((2, width // 4, deep), BF16),
            jax.ShapeDtypeStruct((1, deep), F32),
        ],
        scratch_shapes=[pltpu.VMEM((width, rows), BF16)],
        compiler_params=params(),
        cost_estimate=cost(4 * rows * width * deep, 4 * deep * (rows + width) + 4 * rows * width),
        name="up_back",
    )(core, dm, w_down, slope, x)


def norm_back_kernel(
    du_ref, w_ref, out_ref, dh2_ref, hat_ref, rstd_ref, g_ref,
    dh_ref, da_ref, dc_ref, dg_ref, ds_ref, db_ref,
):
    width = dh2_ref.shape[1]
    dn = dh2_ref[...]
    size = width // CHUNKS
    for j in range(du_ref.shape[1] // width):
        w = w_ref[:, j * size : (j + 1) * size, :].reshape(width, width)
        dn = dn + dot_t(du_ref[:, j * width : (j + 1) * width], w)
    hat = hat_ref[...]
    wide = dn * g_ref[...]
    mean_a = jnp.mean(wide, axis=-1, keepdims=True)
    mean_b = jnp.mean(wide * hat, axis=-1, keepdims=True)
    dh = rstd_ref[...] * (wide - mean_a - hat * mean_b)
    dh_ref[...] = dh
    da = dh.astype(BF16)
    da_ref[...] = da
    dc_ref[...] = dot_t(da, out_ref[...].reshape(width, width)).astype(BF16)

    @pl.when(pl.program_id(0) == 0)
    def _():
        dg_ref[...] = jnp.zeros_like(dg_ref)
        ds_ref[...] = jnp.zeros_like(ds_ref)
        db_ref[...] = jnp.zeros_like(db_ref)

    dg_ref[...] += jnp.sum(dn * hat, axis=0, keepdims=True)
    ds_ref[...] += jnp.sum(dn, axis=0, keepdims=True)
    db_ref[...] += jnp.sum(da.astype(F32), axis=0, keepdims=True)


def norm_back(du, held, dh2, hat, rstd, gain, block=256):
    rows, width = hat.shape
    deep = du.shape[1]
    vec = full_spec((1, width))
    row = row_spec(block, width)
    return pl.pallas_call(
        norm_back_kernel,
        grid=(rows // block,),
        in_specs=[row_spec(block, deep), up_weight(held), out_weight(held)]
        + [row, row, row_spec(block, 1), vec],
        out_specs=[row, row, row, vec, vec, vec],
        out_shape=[
            jax.ShapeDtypeStruct((rows, width), F32),
            jax.ShapeDtypeStruct((rows, width), BF16),
            jax.ShapeDtypeStruct((rows, width), BF16),
        ]
        + [jax.ShapeDtypeStruct((1, width), F32)] * 3,
        compiler_params=params(),
        cost_estimate=cost(2 * rows * width * deep, 2 * deep * (rows + width) + 14 * rows * width),
        name="norm_back",
    )(du, held, held, dh2, hat, rstd, gain)


def input_back_kernel(*refs):
    *parts, w_ref, dh_ref, o_ref = refs
    width = o_ref.shape[1]
    total = dh_ref[...]
    for which in range(3):
        pieces = [
            ref[:, at : at + 128]
            for ref in parts
            for at in range(which * 128, ref.shape[1], 384)
        ]
        col = which * width
        total = total + dot_t(jnp.concatenate(pieces, axis=1), w_ref[:, col : col + width])
    o_ref[...] = total.astype(BF16)


def input_back(parts, w, dh, block=256):
    rows, width = dh.shape
    return pl.pallas_call(
        input_back_kernel,
        grid=(rows // block,),
        in_specs=[row_spec(block, p.shape[1]) for p in parts]
        + [pl.BlockSpec((width, 3 * width), lambda i: (0, 0)), row_spec(block, width)],
        out_specs=row_spec(block, width),
        out_shape=jax.ShapeDtypeStruct((rows, width), BF16),
        compiler_params=params(),
        cost_estimate=cost(6 * rows * width * width, 18 * rows * width),
        name="input_back",
    )(*parts, w, dh)


def exchange(x, n, mask):
    return lax.ppermute(x, "dp", [(i, i ^ mask) for i in range(n)])


def pick(x, axis, index):
    return lax.dynamic_index_in_dim(x, index, axis, keepdims=False)


def tie(*values):
    return lax.optimization_barrier(values)


class Scatter:
    def __init__(self, keep, send, n, r):
        self.n, self.h, self.me, self.cols = n, r // 2, lax.axis_index("dp"), keep.shape[-1]
        self.keep, self.got = keep, exchange(send, n, 1)
        self.left = [[4, 3, 2, 1], [4, 3, 2, 1]]
        self.step = 0

    def part(self, side, bit, which):
        left = self.left[side]
        at, size = left.index(bit), 1 << len(left)
        shape = (1 << at, 2, size >> (at + 1), self.h, self.cols)
        total = None
        for value in self.held[side]:
            lead = value.size // math.prod(shape)
            value = value.reshape(lead, *shape)
            start = (side if lead == 2 else 0, 0, which, 0, 0, 0)
            value = lax.dynamic_slice(value, start, (1, shape[0], 1, *shape[2:])).astype(F32)
            total = value if total is None else total + value
        return total.reshape(size // 2, self.h, self.cols)

    def behind(self, along):
        if self.step == 0:
            flat = tie(self.keep, self.got, *along)
            self.held = [flat[:2]] * 2
            return flat[2:]
        flat = tie(*self.held[0], *self.held[1], *along)
        self.held = [flat[:2], flat[2:4]]
        return flat[4:]

    def halve(self, *along):
        along = self.behind(along)
        bits = ((2, 1), (1, 2))
        sums = []
        for side in range(2):
            bit = bits[side][self.step]
            mine = (self.me >> bit) & 1
            sums += [self.part(side, bit, which).astype(BF16) for which in (1 - mine, mine)]
        *sums, = tie(*sums, *along)
        sums, along = sums[:4], sums[4:]
        for side in range(2):
            bit = bits[side][self.step]
            self.held[side] = (sums[2 * side + 1], exchange(sums[2 * side], self.n, 1 << bit))
            self.left[side].remove(bit)
        self.step += 1
        return along[0] if len(along) == 1 else along

    def column_one(self, *along):
        along = self.behind(along)
        mine = self.me >> 4
        sent, kept = [
            jnp.concatenate([self.part(side, 4, which) for side in range(2)], axis=1).astype(BF16)
            for which in (1 - mine, mine)
        ]
        sent, kept, *along = tie(sent, kept, *along)
        self.pair = (kept, exchange(sent, self.n, 16))
        return along[0] if len(along) == 1 else along

    def column_two(self, *along):
        *self.pair, = tie(*self.pair, *along)
        self.pair, along = self.pair[:2], self.pair[2:]
        mine = (self.me >> 3) & 1
        sent, kept = [
            sum(pick(value, 0, which).astype(F32) for value in self.pair) for which in (1 - mine, mine)
        ]
        sent, kept, *along = tie(sent.astype(BF16), kept, *along)
        self.last = [kept, exchange(sent, self.n, 8)]
        return along[0] if len(along) == 1 else along

    def column(self, *along):
        along = self.behind(along)
        mine = self.me >> 3
        sums = [
            jnp.concatenate(
                [
                    sum(pick(v, 0, mine ^ k).astype(F32) for v in self.held[side])
                    for side in range(2)
                ],
                axis=0,
            )
            for k in range(4)
        ]
        *sums, = tie(sums[0], *[v.astype(BF16) for v in sums[1:]], *along)
        sums, along = sums[:4], sums[4:]
        self.last = sums[:1] + [exchange(sums[k], self.n, k << 3) for k in (1, 2, 3)]
        return along[0] if len(along) == 1 else along

    def after(self, *along):
        flat = tie(*self.last, *along)
        self.last, along = flat[: len(self.last)], flat[len(self.last) :]
        return along[0] if len(along) == 1 else along

    def result(self):
        return sum(value.astype(F32) for value in self.last)


class PlainScatter:
    def __init__(self, keep, send, n, r):
        self.keep = keep
        whole = join(keep, send, keep.shape[1] * 4 // CHUNKS)
        self.total = lax.psum_scatter(whole.astype(F32), "dp", scatter_dimension=0, tiled=True)

    def halve(self, *along):
        return along[0] if len(along) == 1 else along

    column = column_one = column_two = after = halve

    def result(self):
        return self.total


def gather(x):
    return lax.all_gather(x, "dp", axis=0, tiled=True)


class Gather:
    def __init__(self, x, n):
        self.n, self.shape = n, x.shape
        self.near = [x] + [exchange(x, n, k << 3) for k in (1, 2, 3)]

    def after(self, *along):
        flat = tie(*self.near, *along)
        self.near = flat[: len(self.near)]
        along = flat[len(self.near) :]
        return along[0] if len(along) == 1 else along

    def column(self, *along):
        h = self.shape[0] // 2
        sides = [jnp.concatenate([v[at : at + h] for v in self.near], axis=0) for at in (0, h)]
        *sides, = tie(*sides, *along)
        self.near = [sides[0], exchange(sides[0], self.n, 2), sides[1], exchange(sides[1], self.n, 4)]
        along = sides[2:]
        return along[0] if len(along) == 1 else along

    def join(self):
        return [jnp.concatenate(self.near[k : k + 2], axis=0) for k in (0, 2)]

    def plane(self, *along):
        sides = self.join()
        *sides, = tie(*sides, *along)
        self.near = [sides[0], exchange(sides[0], self.n, 4), sides[1], exchange(sides[1], self.n, 2)]
        along = sides[2:]
        return along[0] if len(along) == 1 else along

    def pair(self, *along):
        sides = self.join()
        *sides, = tie(*sides, *along)
        pieces = sides[:2] + [exchange(v, self.n, 1) for v in sides[:2]]
        pieces = [v.reshape(16, self.shape[0] // 2, self.shape[1]) for v in pieces]
        return pieces, *sides[2:]


def plain_pieces(whole, size):
    chips = whole.reshape(4, 2, 2, 2, 2, size // 2, whole.shape[1])
    upper = chips[:, :, :, :, 0].transpose(3, 1, 2, 0, 4, 5)
    lower = chips[:, :, :, :, 1].transpose(3, 2, 1, 0, 4, 5)
    return [v[core].reshape(16, size // 2, -1) for core in range(2) for v in (upper, lower)]


def columns(vector, r):
    return vector.reshape(-1, r).T


def table_of(vectors, n, r):
    parts = [v.reshape(n, -1, r).transpose(0, 2, 1).reshape(n * r, -1) for v in vectors]
    return jnp.concatenate(parts, axis=1)


def local(
    n,
    tokens,
    cotangent,
    w_qkv,
    q_bias,
    v_bias,
    w_out,
    out_bias,
    attn_gain,
    attn_shift,
    w_up,
    up_bias,
    w_down,
    down_bias,
    mlp_gain,
    mlp_shift,
):
    rows, width = tokens.shape
    r = w_qkv.shape[0]
    wide = w_up.shape[1] // width
    vectors = (
        q_bias, v_bias, out_bias, attn_gain, attn_shift, down_bias, mlp_gain, mlp_shift, up_bias,
    )
    small = jnp.concatenate([columns(v, r) for v in vectors], axis=1)
    small = jnp.pad(small, ((0, 0), (0, 128 - small.shape[1])))
    first = jnp.concatenate([w_qkv, small], axis=1)
    tokens_t = tokens.T
    core, me, pairs = jnp.int32(0), jnp.int32(0), width // 128
    if n == CHUNKS:
        scatter, me = Scatter, lax.axis_index("dp")
        core = me & 1
        blocks = [w_up[:, j * width : (j + 1) * width] for j in range(wide)]
        others = jnp.concatenate(blocks + [w_out], axis=0)
        first = Gather(first, n)
        others = first.after(others)
        first.column()
        held = gather(others).reshape(CHUNKS, -1, width)
        first.plane()
        pieces, tokens_t, w_down_share = first.pair(tokens_t, w_down)
        second = Gather(w_down_share, n)
    else:
        scatter = PlainScatter
        up = gather(w_up).reshape(CHUNKS, width // CHUNKS, wide, width).transpose(0, 2, 1, 3)
        up = up.reshape(CHUNKS, wide * width // CHUNKS, width)
        out = gather(w_out).reshape(CHUNKS, width // CHUNKS, width)
        held = jnp.concatenate([up, out], axis=1)
        pieces = plain_pieces(gather(first), width // CHUNKS)
        down_pieces = plain_pieces(gather(w_down), wide * width // CHUNKS)
    core, me = core.reshape(1), me.reshape(1)

    qkv, w_full, table = project(me, tokens, pieces)
    ob, g1, s1, db, g2, s2 = [table[j : j + 1] for j in range(2, 8)]
    ub = table[8 : 8 + wide].reshape(wide, CHUNKS, -1).transpose(1, 0, 2).reshape(1, -1)
    half = pairs // 2
    ctx, lse = attend(qkv, width, 0, half)
    if n == CHUNKS:
        ctx = second.column(second.after(ctx))
    ctx, lse = attend(qkv, width, half, pairs - half, (ctx, lse))
    if n == CHUNKS:
        ctx = second.plane(second.after(ctx))
    hat1, rstd1, n1_low = out_norm(ctx, held, ob, tokens, g1, s1)
    act, slope = up_gelu(n1_low, held, ub, 0)
    if n == CHUNKS:
        down_pieces, act = second.pair(second.after(act))
    act, slope = up_gelu(n1_low, held, ub, 1, (act, slope))
    layer_out, dh2, dm, d_g2, d_s2, d_db, full_down = down_norm(
        me, down_pieces, act, db, hat1, g1, s1, g2, s2, cotangent
    )

    sums = {}

    def at(name, *along):
        for who, step in PLAN[name]:
            along = getattr(sums[who], step)(*along)
            along = along if type(along) in (tuple, list) else (along,)
        return along

    def back(k):
        return attend_back(qkv, ctx, dctx, lse, width, sum(PARTS[:k]), PARTS[k])

    sums["D"] = scatter(*down_grad(core, act, dm), n, w_down.shape[0])
    du, keep, send, d_ub = up_back(core, dm, full_down, slope, n1_low)
    sums["U"] = scatter(keep, send, n, r)
    (du,) = at("up_back", du)
    dh1, da, dctx, d_g1, d_s1, d_ob = norm_back(du, held, dh2, hat1, rstd1, g1)
    (dctx,) = at("norm_back", dctx)
    first, sq0, sv0 = back(0)
    (first,) = at("first", first)
    keep, send = attn_grad(core, tokens_t, [first], [ctx, da], "out")
    sums["E"] = scatter(keep, send, n, r)
    keep, dctx = at("early", sums["E"].keep, dctx)
    sums["E"].keep = keep
    second, sq1, sv1 = back(1)
    second, dctx = at("second", second, dctx)
    third, sq2, sv2 = back(2)
    (third,) = at("third", third)
    d_qb = jnp.concatenate([sq0, sq1, sq2], axis=1)
    d_vb = jnp.concatenate([sv0, sv1, sv2], axis=1)
    d_small = table_of([d_qb, d_vb, d_ob, d_g1, d_s1, d_db, d_g2, d_s2, d_ub], CHUNKS, width // CHUNKS)
    d_small = jnp.pad(d_small, ((0, 0), (0, 128 - d_small.shape[1]))).astype(BF16)
    keep, send = attn_grad(core, tokens_t, [second, third], [d_small], "small")
    sums["L"] = scatter(keep, send, n, r)
    keep, dh1 = at("late", sums["L"].keep, dh1)
    sums["L"].keep = keep
    input_grad = input_back([first, second, third], w_full, dh1)
    (input_grad,) = at("input_back", input_grad)
    down_sum, up_sum, early_sum, late_sum = [sums[k] for k in "DUEL"]

    early, late = early_sum.result(), late_sum.result()
    qkv_cols = PARTS[0] * 384
    d_qkv = jnp.concatenate([early[:, :qkv_cols], late[:, : 3 * width - qkv_cols]], axis=1)
    d_qkv = d_qkv.reshape(r, pairs, 3, 128).transpose(0, 2, 1, 3).reshape(r, 3 * width)
    d_out = early[:, qkv_cols:]
    d_small = late[:, 3 * width - qkv_cols :]

    def vector(start, k=1):
        return d_small[:, start : start + k].T.reshape(-1)

    d_qb, d_vb, d_ob, d_g1, d_s1, d_db, d_g2, d_s2 = [vector(j) for j in range(8)]
    d_ub = d_small[:, 8 : 8 + wide]
    d_ub = d_ub.T.reshape(-1)
    return (
        layer_out, input_grad, d_qkv, d_qb, d_vb, d_out, d_ob, d_g1, d_s1,
        up_sum.result(), d_ub, down_sum.result(), d_db, d_g2, d_s2,
    )


def solution(mesh):
    flat, square = P("dp"), P("dp", None)
    in_specs = (
        square, square, square, flat, flat, square, flat, flat, flat,
        square, flat, square, flat, flat, flat,
    )
    return jax.shard_map(
        functools.partial(local, mesh.shape["dp"]),
        mesh=mesh,
        in_specs=in_specs,
        out_specs=in_specs,
        check_vma=False,
    )
```
